32 devices in a mesh: wide: 8 (over z, y), narrow: 4 (over x, core).
Axes of the slice: x: 2, y: 2, z: 4, core: 2. Of those that a mesh axis runs over, the one named last changes fastest.
Arguments:
- stored_features: bfloat16 [64, 16, 16, 128], P(None, 'wide', 'narrow'), may hold values from -127 to 127
- channel_scale: float32 [64], replicated, may hold values from 0.005 to 0.05
- channel_shift: float32 [64], replicated, may hold values from -0.5 to 0.5
- first_weight: bfloat16 [64, 1728], replicated, may hold values from -0.21875 to 0.21875
- second_weight: bfloat16 [128, 1728], replicated, may hold values from -0.21875 to 0.21875
- third_weight: bfloat16 [256, 3456], P('narrow'), may hold values from -0.15625 to 0.15625
Outputs:
- coarse_features: bfloat16 [256, 8, 512], P('narrow', 'wide')
The draws below stay inside these ranges and needn't reach their ends.
All inputs are finite; a program needn't handle non-finite values.
Results may differ from the reference program's by a relative error of at most 0.0057.
Values may be sent and summed in bfloat16 or wider, within the bound.
No kernel may reach another device: no remote copies, remote signals or barrier semaphores. Data moves between devices by JAX's collectives and lax.ppermute only.
A program may use at most 64 MiB of HBM per device.

```python
import math
import jax
import jax.numpy as jnp
from jax import lax

C1 = 64
C2 = 128
C3 = 256
LEN_W = 128
ND = 16
NH = 16


def level_of(rng, dims, shards, least, largest):
    def one(dim, blocks):
        heights = jax.random.uniform(jax.random.fold_in(jax.random.fold_in(rng, 6), dim), (blocks,), jnp.float32, least / len(shards), largest / len(shards))
        return jnp.repeat(jnp.exp(heights), dims[dim] // blocks).reshape((-1,) + (1,) * (len(dims) - dim - 1))

    gain = one(*shards[0])
    for cut in shards[1:]:
        gain = gain * one(*cut)
    return gain


def normal_values(stream_key, extent, deviation, bound, split=(), kind=jnp.bfloat16):
    values = jax.random.normal(stream_key, extent, jnp.float32) * deviation
    if len(split) > 0:
        values = level_of(stream_key, extent, split, -0.22, 0.18) * values
    return jnp.clip(values, min=-bound, max=bound).astype(kind)


def setup_inputs(seed: int = 0) -> dict:
    keys = jax.random.split(jax.random.key(seed), 7)
    stored_features = normal_values(keys[0], (C1, ND, NH, LEN_W), 40.0, 127.0, ((1, 8), (2, 4)))
    channel_scale = jnp.clip(jnp.exp(jax.random.uniform(keys[1], (C1,), jnp.float32, math.log(0.005), math.log(0.05))), 0.005, 0.05)
    channel_shift = jnp.clip(jax.random.uniform(keys[2], (C1,), jnp.float32, -0.5, 0.5), -0.5, 0.5)
    first_weight = normal_values(keys[3], (C1, 27 * C1), (27 * C1 // 2) ** -0.5, 0.21875)
    second_weight = normal_values(keys[4], (C2, 27 * C1), (27 * C1 // 2) ** -0.5, 0.21875)
    third_weight = normal_values(keys[5], (C3, 27 * C2), (27 * C2 // 2) ** -0.5, 0.15625, ((0, 4),))
    return {"stored_features": stored_features, "channel_scale": channel_scale, "channel_shift": channel_shift, "first_weight": first_weight, "second_weight": second_weight, "third_weight": third_weight}


def convolve(features, weight):
    out_channels = weight.shape[0]
    in_channels = features.shape[0]
    kernel = weight.astype(jnp.float32).reshape(out_channels, 3, 3, 3, in_channels).transpose(0, 4, 1, 2, 3)
    result = lax.conv_general_dilated(features.astype(jnp.float32)[None], kernel, (1, 1, 1), ((1, 1), (1, 1), (1, 1)), dimension_numbers=("NCDHW", "OIDHW", "NCDHW"), precision=lax.Precision.HIGHEST)
    return result[0]


def reference(stored_features, channel_scale, channel_shift, first_weight, second_weight, third_weight):
    features = (stored_features.astype(jnp.float32) * channel_scale[:, None, None, None] + channel_shift[:, None, None, None]).astype(jnp.bfloat16)
    first_hidden = jnp.maximum(convolve(features, first_weight), 0.0).astype(jnp.bfloat16)
    second_hidden = jnp.maximum(convolve(first_hidden, second_weight), 0.0).astype(jnp.bfloat16)
    channels, depth_cells, height_cells, width_cells = second_hidden.shape
    pooled = second_hidden.reshape(channels, depth_cells // 2, 2, height_cells // 2, 2, width_cells // 2, 2).max(axis=(2, 4, 6))
    coarse = jnp.maximum(convolve(pooled, third_weight), 0.0).astype(jnp.bfloat16)
    return coarse.reshape(coarse.shape[0], coarse.shape[1], -1)
```

```python
import functools

import jax
import jax.numpy as jnp
from jax import lax
from jax.experimental import pallas as pl
from jax.experimental.pallas import tpu as pltpu
from jax.sharding import PartitionSpec as P

LANES = 128
VMEM = pl.BlockSpec(memory_space=pltpu.VMEM)


def pair_swap(count, bit=1):
    return [(k, k ^ bit) for k in range(count)]


def pair_relay(count):
    steps = []
    for k in range(count):
        target = k - 2 if k % 2 == 0 else k + 2
        steps.append((k, target if 0 <= target < count else k ^ 1))
    return steps


def pair_relay_back(count):
    return [(target, source) for source, target in pair_relay(count)]


def weights_kernel(w1_ref, w2_ref, w3_ref, t1_ref, t2_ref, t3_ref):
    o1 = w1_ref.shape[0]
    c1 = w1_ref.shape[1] // 27
    o2 = w2_ref.shape[0]
    c2 = w2_ref.shape[1] // 27
    o3 = w3_ref.shape[0]
    c3 = w3_ref.shape[1] // 27
    for ref, out, o, c, rows in ((w1_ref, t1_ref, o1, c1, 4), (w2_ref, t2_ref, o2, c2, 2)):
        span = (rows + 2) * c
        for be in range(9):
            taps = [ref[:, (a * 9 + be) * c : (a * 9 + be + 1) * c] for a in range(3)]
            for row in range(rows):
                parts = []
                if row:
                    parts.append(jnp.zeros((o, row * c), jnp.bfloat16))
                parts += taps
                if row < rows - 1:
                    parts.append(jnp.zeros((o, (rows - 1 - row) * c), jnp.bfloat16))
                out[row * o : (row + 1) * o, be * span : (be + 1) * span] = jnp.concatenate(
                    parts, axis=1
                )
    for be in range(9):
        for a in range(3):
            t3_ref[be * o3 : (be + 1) * o3, a * c3 : (a + 1) * c3] = w3_ref[
                :, (a * 9 + be) * c3 : (a * 9 + be + 1) * c3
            ]


def shifted(value):
    lane = lax.broadcasted_iota(jnp.int32, value.shape, 1)
    low = jnp.where(lane == 0, 0.0, pltpu.roll(value, 1, 1))
    high = jnp.where(lane == LANES - 1, 0.0, pltpu.roll(value, LANES - 1, 1))
    return low, value, high


def fine_kernel(
    wide, narrow, channels, own_ref, pair_ref, far_ref, side_ref, scale_ref, shift_ref, w1_ref,
    w2_ref, out_ref, raw, taps, hidden,
):
    c = channels
    i, j = lax.axis_index("wide"), lax.axis_index("narrow")
    i_odd, j_odd = lax.rem(i, 2), lax.rem(j, 2)
    pair_slot, far_slot = 2 - 2 * i_odd, 2 * i_odd
    depth, height = 2, 4
    block = c * depth * height
    raw[0:block, :] = own_ref[...].astype(jnp.float32)
    raw[block : 2 * block, :] = pair_ref[...].astype(jnp.float32)
    raw[2 * block : 3 * block, :] = far_ref[...].astype(jnp.float32)
    raw[3 * block :, :] = side_ref[...].astype(jnp.float32)
    scale, shift = scale_ref[...], shift_ref[...]
    slab = 6 * c

    def put(value, slot, d, lane):
        row = pl.multiple_of(slot * (depth * c) + d * c, c)
        for e, part in enumerate(shifted(value)):
            taps[pl.ds(pl.multiple_of(e * slab + row, c), c), pl.ds(lane, LANES)] = part.astype(
                jnp.bfloat16
            )

    slots = (1, pair_slot, far_slot)
    for k in range(3):
        for d in range(depth):
            for h in range(height):
                rows = raw[pl.ds(k * block + d * height + h, c, stride=depth * height), :]
                put(rows * scale + shift, slots[k], d, (2 + h) * LANES)
    for part in range(2):
        side = (1 - j_odd) if part == 0 else j_odd
        for k in range(3):
            for d in range(depth):
                for h in range(2):
                    start = 3 * block + ((part * 3 + k) * c * depth * 2) + d * 2 + h
                    rows = raw[pl.ds(start, c, stride=depth * 2), :]
                    lane = pl.multiple_of((side * 6 + h) * LANES, LANES)
                    put(rows * scale + shift, slots[k], d, lane)

    zero = functools.partial(jnp.zeros, dtype=jnp.bfloat16)

    @pl.when(i == 0)
    def _():
        for e in range(3):
            taps[e * slab : e * slab + 2 * c, :] = zero((2 * c, 8 * LANES))

    @pl.when(i == wide - 1)
    def _():
        for e in range(3):
            taps[e * slab + 4 * c : (e + 1) * slab, :] = zero((2 * c, 8 * LANES))

    @pl.when(j == 0)
    def _():
        taps[:, 0 : 2 * LANES] = zero((3 * slab, 2 * LANES))

    @pl.when(j == narrow - 1)
    def _():
        taps[:, 6 * LANES :] = zero((3 * slab, 2 * LANES))

    h_slab = 4 * c
    w1 = w1_ref[...]
    for n in range(3):
        columns = jnp.concatenate(
            [taps[:, (2 * n + b) * LANES : (2 * n + b + 2) * LANES] for b in range(3)], axis=0
        )
        result = jnp.maximum(jnp.dot(w1, columns, preferred_element_type=jnp.float32), 0.0)
        for k in range(2):
            lane = (2 * n + k) * LANES
            for e, part in enumerate(shifted(result[:, k * LANES : (k + 1) * LANES])):
                hidden[e * h_slab : (e + 1) * h_slab, lane : lane + LANES] = part.astype(
                    jnp.bfloat16
                )

    @pl.when(i == 0)
    def _():
        for e in range(3):
            hidden[e * h_slab : e * h_slab + c, :] = zero((c, 6 * LANES))

    @pl.when(i == wide - 1)
    def _():
        for e in range(3):
            hidden[e * h_slab + 3 * c : (e + 1) * h_slab, :] = zero((c, 6 * LANES))

    @pl.when(j == 0)
    def _():
        hidden[:, 0:LANES] = zero((3 * h_slab, LANES))

    @pl.when(j == narrow - 1)
    def _():
        hidden[:, 5 * LANES :] = zero((3 * h_slab, LANES))

    w2 = w2_ref[...]
    c2 = out_ref.shape[0]
    cell = lax.broadcasted_iota(jnp.int32, (LANES, LANES), 0)
    target = lax.broadcasted_iota(jnp.int32, (LANES, LANES), 1)
    pooled = None
    for n in range(2):
        columns = jnp.concatenate(
            [hidden[:, (2 * n + b) * LANES : (2 * n + b + 2) * LANES] for b in range(3)], axis=0
        )
        result = jnp.dot(w2, columns, preferred_element_type=jnp.float32)
        best = jnp.maximum(result[0:c2], result[c2:])
        best = jnp.maximum(jnp.maximum(best[:, 0:LANES], best[:, LANES:]), 0.0)
        best = jnp.maximum(best, pltpu.roll(best, LANES - 1, 1)).astype(jnp.bfloat16)
        pick = (cell == 2 * target - n * LANES).astype(jnp.bfloat16)
        moved = jnp.dot(best, pick, preferred_element_type=jnp.float32)
        pooled = moved if pooled is None else pooled + moved
    out_ref[...] = pooled.astype(jnp.bfloat16)


def coarse_kernel(wide, narrow, mine_ref, theirs_ref, w3_ref, out_ref, slab):
    i, j = lax.axis_index("wide"), lax.axis_index("narrow")
    i_odd = lax.rem(i, 2)
    groups, _, c, lanes = mine_ref.shape
    slots = (1, 2 - 2 * i_odd, 2 * i_odd)
    for r in range(groups):
        for bit, ref in ((0, mine_ref), (1, theirs_ref)):
            lane = pl.multiple_of(jnp.bitwise_xor(j, 2 * r + bit) * lanes, lanes)
            for k in range(3):
                row = pl.multiple_of(slots[k] * c, c)
                slab[pl.ds(row, c), pl.ds(lane, lanes)] = ref[r, k]
    total = slab.shape[1]

    @pl.when(i == 0)
    def _():
        slab[0:c, :] = jnp.zeros((c, total), jnp.bfloat16)

    @pl.when(i == wide - 1)
    def _():
        slab[2 * c :, :] = jnp.zeros((c, total), jnp.bfloat16)

    o = out_ref.shape[0]
    width = lanes // 2
    z = jnp.dot(w3_ref[...], slab[...], preferred_element_type=jnp.float32)
    place = lax.broadcasted_iota(jnp.int32, (o, total), 1)
    column = lax.rem(place, width)
    result = None
    for e in range(3):
        low, mid, high = (z[(b * 3 + e) * o : (b * 3 + e + 1) * o] for b in range(3))
        low = jnp.where(place < width, 0.0, pltpu.roll(low, width, 1))
        high = jnp.where(place >= total - width, 0.0, pltpu.roll(high, total - width, 1))
        term = low + mid + high
        if e == 0:
            term = jnp.where(column == 0, 0.0, pltpu.roll(term, 1, 1))
        if e == 2:
            term = jnp.where(column == width - 1, 0.0, pltpu.roll(term, total - 1, 1))
        result = term if result is None else result + term
    out_ref[...] = jnp.maximum(result, 0.0).astype(jnp.bfloat16)


def body(
    wide, narrow, stored_features, channel_scale, channel_shift, first_weight, second_weight,
    third_weight,
):
    c1, depth, height, width = stored_features.shape
    c2 = second_weight.shape[0]
    o3 = third_weight.shape[0]
    params = pltpu.CompilerParams(vmem_limit_bytes=24 * 1024 * 1024)
    j_odd = lax.axis_index("narrow") % 2 == 1

    pair = lax.ppermute(stored_features, "wide", pair_swap(wide))
    t1, t2, t3 = pl.pallas_call(
        weights_kernel,
        out_shape=(
            jax.ShapeDtypeStruct((4 * c1, 9 * 6 * c1), jnp.bfloat16),
            jax.ShapeDtypeStruct((2 * c2, 9 * 4 * c1), jnp.bfloat16),
            jax.ShapeDtypeStruct((9 * o3, 3 * c2), jnp.bfloat16),
        ),
        in_specs=[VMEM] * 3,
        out_specs=(VMEM,) * 3,
        compiler_params=params,
        cost_estimate=pl.CostEstimate(flops=10**6, bytes_accessed=4 * 10**6, transcendentals=0),
    )(first_weight, second_weight, third_weight)
    far = lax.ppermute(pair, "wide", pair_relay_back(wide))
    half = height // 2
    blocks = jnp.stack([stored_features, pair, far])
    first_rows, last_rows = blocks[:, :, :, :half], blocks[:, :, :, half:]
    relayed = lax.ppermute(
        jnp.where(j_odd, last_rows, first_rows), "narrow", pair_relay(narrow)
    )
    side = lax.ppermute(
        jnp.stack([jnp.where(j_odd, first_rows, last_rows), relayed]), "narrow", pair_swap(narrow)
    )
    rows = c1 * depth * height
    pooled = pl.pallas_call(
        functools.partial(fine_kernel, wide, narrow, c1),
        out_shape=jax.ShapeDtypeStruct((c2, LANES), jnp.bfloat16),
        in_specs=[VMEM] * 8,
        out_specs=VMEM,
        scratch_shapes=[
            pltpu.VMEM((6 * rows, width), jnp.float32),
            pltpu.VMEM((18 * c1, 8 * width), jnp.bfloat16),
            pltpu.VMEM((12 * c1, 6 * width), jnp.bfloat16),
        ],
        compiler_params=params,
        cost_estimate=pl.CostEstimate(
            flops=2 * 10**9, bytes_accessed=4 * 10**6, transcendentals=0
        ),
    )(
        stored_features.reshape(rows, width),
        pair.reshape(rows, width),
        far.reshape(rows, width),
        side.reshape(3 * rows, width),
        channel_scale.reshape(c1, 1),
        channel_shift.reshape(c1, 1),
        t1,
        t2,
    )
    pooled_pair = lax.ppermute(pooled, "wide", pair_swap(wide))
    pooled_far = lax.ppermute(pooled_pair, "wide", pair_relay_back(wide))
    mine = jnp.stack([pooled, pooled_pair, pooled_far])[None]
    bit = narrow // 2
    while bit > 1:
        other = lax.ppermute(mine, "narrow", pair_swap(narrow, bit))
        mine = jnp.stack([mine, other], axis=1).reshape((-1,) + mine.shape[1:])
        bit //= 2
    theirs = lax.ppermute(mine, "narrow", pair_swap(narrow))
    total = narrow * LANES
    coarse = pl.pallas_call(
        functools.partial(coarse_kernel, wide, narrow),
        out_shape=jax.ShapeDtypeStruct((o3, total), jnp.bfloat16),
        in_specs=[VMEM] * 3,
        out_specs=VMEM,
        scratch_shapes=[pltpu.VMEM((3 * c2, total), jnp.bfloat16)],
        compiler_params=params,
        cost_estimate=pl.CostEstimate(flops=10**9, bytes_accessed=10**6, transcendentals=0),
    )(mine, theirs, t3)
    return coarse[:, None, :]


def solution(mesh):
    in_specs = (P(None, "wide", "narrow", None), P(), P(), P(), P(), P("narrow", None))
    out_specs = P("narrow", "wide", None)
    return jax.shard_map(
        functools.partial(body, mesh.shape["wide"], mesh.shape["narrow"]),
        mesh=mesh,
        in_specs=in_specs,
        out_specs=out_specs,
        check_vma=False,
    )
```

```python
import functools

import jax
import jax.numpy as jnp
from jax import lax
from jax.experimental import pallas as pl
from jax.experimental.pallas import tpu as pltpu
from jax.sharding import PartitionSpec as P

LANES = 128
VMEM = pl.BlockSpec(memory_space=pltpu.VMEM)


def pair_swap(count, bit=1):
    return [(k, k ^ bit) for k in range(count)]


def pair_relay(count):
    steps = []
    for k in range(count):
        target = k - 2 if k % 2 == 0 else k + 2
        steps.append((k, target if 0 <= target < count else k ^ 1))
    return steps


def pair_relay_back(count):
    return [(target, source) for source, target in pair_relay(count)]


def weights_kernel(w1_ref, w2_ref, w3_ref, t1_ref, t2_ref, t3_ref):
    o1 = w1_ref.shape[0]
    c1 = w1_ref.shape[1] // 27
    o2 = w2_ref.shape[0]
    c2 = w2_ref.shape[1] // 27
    o3 = w3_ref.shape[0]
    c3 = w3_ref.shape[1] // 27
    for ref, out, o, c, rows in ((w1_ref, t1_ref, o1, c1, 4), (w2_ref, t2_ref, o2, c2, 2)):
        span = (rows + 2) * c
        for be in range(9):
            taps = [ref[:, (a * 9 + be) * c : (a * 9 + be + 1) * c] for a in range(3)]
            for row in range(rows):
                parts = []
                if row:
                    parts.append(jnp.zeros((o, row * c), jnp.bfloat16))
                parts += taps
                if row < rows - 1:
                    parts.append(jnp.zeros((o, (rows - 1 - row) * c), jnp.bfloat16))
                out[row * o : (row + 1) * o, be * span : (be + 1) * span] = jnp.concatenate(
                    parts, axis=1
                )
    for be in range(9):
        for a in range(3):
            t3_ref[be * o3 : (be + 1) * o3, a * c3 : (a + 1) * c3] = w3_ref[
                :, (a * 9 + be) * c3 : (a * 9 + be + 1) * c3
            ]


def shifted(value):
    lane = lax.broadcasted_iota(jnp.int32, value.shape, 1)
    low = jnp.where(lane == 0, 0.0, pltpu.roll(value, 1, 1))
    high = jnp.where(lane == LANES - 1, 0.0, pltpu.roll(value, LANES - 1, 1))
    return low, value, high


def unpack_kernel(raw_ref, scale_ref, shift_ref, out_ref, staged):
    c = scale_ref.shape[0]
    depth, height = out_ref.shape[0] // c, out_ref.shape[1] // LANES
    staged[...] = raw_ref[...].astype(jnp.float32)
    scale, shift = scale_ref[...], shift_ref[...]
    for d in range(depth):
        for h in range(height):
            rows = staged[pl.ds(d * height + h, c, stride=depth * height), :]
            out_ref[d * c : (d + 1) * c, h * LANES : (h + 1) * LANES] = (
                rows * scale + shift
            ).astype(jnp.bfloat16)


def slab_kernel(
    wide, raw_ref, scale_ref, shift_ref, own_ref, pair_ref, out_ref, relay_ref, side_ref, staged
):
    i, j = lax.axis_index("wide"), lax.axis_index("narrow")
    i_odd, j_odd = lax.rem(i, 2), lax.rem(j, 2)
    block, columns = own_ref.shape
    c = scale_ref.shape[0]
    depth, height = block // c, columns // LANES
    far_row = pl.multiple_of(2 * i_odd * block, block)
    pair_row = pl.multiple_of((2 - 2 * i_odd) * block, block)
    staged[...] = raw_ref[...].astype(jnp.float32)
    scale, shift = scale_ref[...], shift_ref[...]
    for d in range(depth):
        for h in range(height):
            rows = staged[pl.ds(d * height + h, c, stride=depth * height), :]
            out_ref[
                pl.ds(pl.multiple_of(far_row + d * c, c), c), h * LANES : (h + 1) * LANES
            ] = (rows * scale + shift).astype(jnp.bfloat16)

    @pl.when(jnp.where(i_odd == 0, i == 0, i == wide - 1))
    def _():
        out_ref[pl.ds(far_row, block), :] = jnp.zeros((block, columns), jnp.bfloat16)

    out_ref[block : 2 * block, :] = own_ref[...]
    out_ref[pl.ds(pair_row, block), :] = pair_ref[...]
    half = columns // 2
    relay_ref[...] = out_ref[:, pl.ds(pl.multiple_of(j_odd * half, half), half)]
    side_ref[...] = out_ref[:, pl.ds(pl.multiple_of((1 - j_odd) * half, half), half)]


def dot(a, b):
    return jnp.dot(a, b, preferred_element_type=jnp.float32)


def tile(ref, *picks):
    return jnp.concatenate([ref[:, k * LANES : (k + 1) * LANES] for k in picks], axis=1)


def spread(value, ref, at):
    rows, columns = value.shape
    for k in range(columns // LANES):
        parts = shifted(value[:, k * LANES : (k + 1) * LANES].astype(jnp.float32))
        for e, part in enumerate(parts):
            ref[e * rows : (e + 1) * rows, pl.ds(at + k * LANES, LANES)] = part.astype(jnp.bfloat16)


def clear_depth(wide, ref):
    i = lax.axis_index("wide")
    span = ref.shape[0] // 3
    c = span // 4

    @pl.when(i == 0)
    def _():
        for e in range(3):
            ref[e * span : e * span + c, :] = jnp.zeros((c, ref.shape[1]), jnp.bfloat16)

    @pl.when(i == wide - 1)
    def _():
        for e in range(3):
            ref[e * span + 3 * c : (e + 1) * span, :] = jnp.zeros((c, ref.shape[1]), jnp.bfloat16)


def thirds(ref):
    span = ref.shape[1] // 3
    return [ref[:, b * span : (b + 1) * span] for b in range(3)]


def centre_kernel(wide, x_ref, w1_ref, w2_ref, p1_ref, p2_ref, taps, hidden):
    spread(x_ref[...], taps, 0)
    first = thirds(w1_ref)
    columns = jnp.concatenate(
        [taps[:, b * LANES : (b + 2) * LANES] for b in range(3)], axis=0
    )
    spread(jnp.maximum(dot(w1_ref[...], columns), 0.0), hidden, 0)
    clear_depth(wide, hidden)
    r0 = dot(first[0], tile(taps, 2, 3))
    r1 = dot(first[1], tile(taps, 0, 3))
    r2 = dot(first[2], tile(taps, 0, 1))
    p1_ref[:, 0:LANES] = r2[:, :LANES]
    p1_ref[:, LANES : 2 * LANES] = r2[:, LANES:] + r1[:, :LANES]
    p1_ref[:, 2 * LANES : 3 * LANES] = r1[:, LANES:] + r0[:, :LANES]
    p1_ref[:, 3 * LANES :] = r0[:, LANES:]
    both = hidden[...]
    q0, q1, q2 = (dot(w, both) for w in thirds(w2_ref))
    p2_ref[:, 0:LANES] = q2[:, :LANES]
    p2_ref[:, LANES : 2 * LANES] = q2[:, LANES:] + q1[:, :LANES]
    p2_ref[:, 2 * LANES : 3 * LANES] = q1[:, LANES:] + q0[:, :LANES]
    p2_ref[:, 3 * LANES :] = q0[:, LANES:]


def edge_kernel(
    wide, narrow, partner_ref, relayed_ref, p1_ref, p2_ref, w1_ref, w2_ref, out_ref, taps, hidden
):
    j = lax.axis_index("narrow")
    j_odd = lax.rem(j, 2)
    half = partner_ref.shape[1]
    spread(partner_ref[...], taps, pl.multiple_of((1 - j_odd) * half, half))
    spread(relayed_ref[...], taps, pl.multiple_of(j_odd * half, half))

    @pl.when(j == 0)
    def _():
        taps[:, :half] = jnp.zeros((taps.shape[0], half), jnp.bfloat16)

    @pl.when(j == narrow - 1)
    def _():
        taps[:, half:] = jnp.zeros((taps.shape[0], half), jnp.bfloat16)

    first = thirds(w1_ref)
    r0 = dot(first[0], tile(taps, 0, 1))
    r1 = dot(first[1], tile(taps, 1, 2))
    r2 = dot(first[2], tile(taps, 2, 3))
    rows = (
        r0[:, :LANES] + r1[:, :LANES],
        r0[:, LANES:],
        r2[:, :LANES],
        r1[:, LANES:] + r2[:, LANES:],
    )
    for k, value in enumerate(rows):
        spread(
            jnp.maximum(value + p1_ref[:, k * LANES : (k + 1) * LANES], 0.0), hidden, k * LANES
        )
    clear_depth(wide, hidden)

    @pl.when(j == 0)
    def _():
        hidden[:, :LANES] = jnp.zeros((hidden.shape[0], LANES), jnp.bfloat16)

    @pl.when(j == narrow - 1)
    def _():
        hidden[:, 3 * LANES :] = jnp.zeros((hidden.shape[0], LANES), jnp.bfloat16)

    second = thirds(w2_ref)
    q0 = dot(second[0], tile(hidden, 0, 1))
    q1 = dot(second[1], tile(hidden, 1, 2))
    q2 = dot(second[2], tile(hidden, 2, 3))
    outs = (
        q0[:, :LANES] + q1[:, :LANES],
        q0[:, LANES:],
        q2[:, :LANES],
        q1[:, LANES:] + q2[:, LANES:],
    )
    outs = [value + p2_ref[:, k * LANES : (k + 1) * LANES] for k, value in enumerate(outs)]
    c2 = out_ref.shape[0]
    best = []
    for n in range(2):
        value = jnp.maximum(outs[2 * n], outs[2 * n + 1])
        value = jnp.maximum(jnp.maximum(value[:c2], value[c2:]), 0.0)
        best.append(jnp.maximum(value, pltpu.roll(value, LANES - 1, 1)).astype(jnp.bfloat16))
    cell = lax.broadcasted_iota(jnp.int32, (2 * LANES, LANES), 0)
    target = lax.broadcasted_iota(jnp.int32, (2 * LANES, LANES), 1)
    pick = (cell == 2 * target).astype(jnp.bfloat16)
    out_ref[...] = dot(jnp.concatenate(best, axis=1), pick).astype(jnp.bfloat16)


def coarse_kernel(wide, narrow, mine_ref, theirs_ref, w3_ref, out_ref, slab):
    i, j = lax.axis_index("wide"), lax.axis_index("narrow")
    i_odd = lax.rem(i, 2)
    groups, _, c, lanes = mine_ref.shape
    slots = (1, 2 - 2 * i_odd, 2 * i_odd)
    for r in range(groups):
        for bit, ref in ((0, mine_ref), (1, theirs_ref)):
            lane = pl.multiple_of(jnp.bitwise_xor(j, 2 * r + bit) * lanes, lanes)
            for k in range(3):
                row = pl.multiple_of(slots[k] * c, c)
                slab[pl.ds(row, c), pl.ds(lane, lanes)] = ref[r, k]
    total = slab.shape[1]

    @pl.when(i == 0)
    def _():
        slab[0:c, :] = jnp.zeros((c, total), jnp.bfloat16)

    @pl.when(i == wide - 1)
    def _():
        slab[2 * c :, :] = jnp.zeros((c, total), jnp.bfloat16)

    o = out_ref.shape[0]
    width = lanes // 2
    z = jnp.dot(w3_ref[...], slab[...], preferred_element_type=jnp.float32)
    place = lax.broadcasted_iota(jnp.int32, (o, total), 1)
    column = lax.rem(place, width)
    result = None
    for e in range(3):
        low, mid, high = (z[(b * 3 + e) * o : (b * 3 + e + 1) * o] for b in range(3))
        low = jnp.where(place < width, 0.0, pltpu.roll(low, width, 1))
        high = jnp.where(place >= total - width, 0.0, pltpu.roll(high, total - width, 1))
        term = low + mid + high
        if e == 0:
            term = jnp.where(column == 0, 0.0, pltpu.roll(term, 1, 1))
        if e == 2:
            term = jnp.where(column == width - 1, 0.0, pltpu.roll(term, total - 1, 1))
        result = term if result is None else result + term
    out_ref[...] = jnp.maximum(result, 0.0).astype(jnp.bfloat16)


def body(
    wide, narrow, stored_features, channel_scale, channel_shift, first_weight, second_weight,
    third_weight,
):
    c1, depth, height, width = stored_features.shape
    c2 = second_weight.shape[0]
    o3 = third_weight.shape[0]
    params = pltpu.CompilerParams(vmem_limit_bytes=24 * 1024 * 1024)
    rows = c1 * depth * height
    columns = height * width
    scale, shift = channel_scale.reshape(c1, 1), channel_shift.reshape(c1, 1)

    def cost(flops, size):
        return pl.CostEstimate(flops=flops, bytes_accessed=size, transcendentals=0)

    def unpack(block):
        return pl.pallas_call(
            unpack_kernel,
            out_shape=jax.ShapeDtypeStruct((depth * c1, columns), jnp.bfloat16),
            in_specs=[VMEM] * 3,
            out_specs=VMEM,
            scratch_shapes=[pltpu.VMEM((rows, width), jnp.float32)],
            compiler_params=params,
            cost_estimate=cost(10**6, 10**6),
        )(block.reshape(rows, width), scale, shift)

    pair = lax.ppermute(stored_features, "wide", pair_swap(wide))
    t1, t2, t3 = pl.pallas_call(
        weights_kernel,
        out_shape=(
            jax.ShapeDtypeStruct((4 * c1, 9 * 6 * c1), jnp.bfloat16),
            jax.ShapeDtypeStruct((2 * c2, 9 * 4 * c1), jnp.bfloat16),
            jax.ShapeDtypeStruct((9 * o3, 3 * c2), jnp.bfloat16),
        ),
        in_specs=[VMEM] * 3,
        out_specs=(VMEM,) * 3,
        compiler_params=params,
        cost_estimate=cost(10**6, 4 * 10**6),
    )(first_weight, second_weight, third_weight)
    own_slab = unpack(stored_features)
    far = lax.ppermute(pair, "wide", pair_relay_back(wide))
    pair_slab = unpack(pair)
    slab, relay, side = pl.pallas_call(
        functools.partial(slab_kernel, wide),
        out_shape=(
            jax.ShapeDtypeStruct((6 * c1, columns), jnp.bfloat16),
            jax.ShapeDtypeStruct((6 * c1, columns // 2), jnp.bfloat16),
            jax.ShapeDtypeStruct((6 * c1, columns // 2), jnp.bfloat16),
        ),
        in_specs=[VMEM] * 5,
        out_specs=(VMEM,) * 3,
        scratch_shapes=[pltpu.VMEM((rows, width), jnp.float32)],
        compiler_params=params,
        cost_estimate=cost(10**6, 2 * 10**6),
    )(far.reshape(rows, width), scale, shift, own_slab, pair_slab)
    passed = lax.ppermute(relay, "narrow", pair_relay(narrow))
    partner_rows = lax.ppermute(side, "narrow", pair_swap(narrow))
    p1, p2 = pl.pallas_call(
        functools.partial(centre_kernel, wide),
        out_shape=(
            jax.ShapeDtypeStruct((4 * c1, 4 * width), jnp.float32),
            jax.ShapeDtypeStruct((2 * c2, 4 * width), jnp.float32),
        ),
        in_specs=[VMEM] * 3,
        out_specs=(VMEM,) * 2,
        scratch_shapes=[
            pltpu.VMEM((18 * c1, 4 * width), jnp.bfloat16),
            pltpu.VMEM((12 * c1, 2 * width), jnp.bfloat16),
        ],
        compiler_params=params,
        cost_estimate=cost(2 * 10**9, 4 * 10**6),
    )(slab, t1, t2)
    relayed_rows = lax.ppermute(passed, "narrow", pair_swap(narrow))
    pooled = pl.pallas_call(
        functools.partial(edge_kernel, wide, narrow),
        out_shape=jax.ShapeDtypeStruct((c2, LANES), jnp.bfloat16),
        in_specs=[VMEM] * 6,
        out_specs=VMEM,
        scratch_shapes=[
            pltpu.VMEM((18 * c1, 4 * width), jnp.bfloat16),
            pltpu.VMEM((12 * c1, 4 * width), jnp.bfloat16),
        ],
        compiler_params=params,
        cost_estimate=cost(10**9, 4 * 10**6),
    )(partner_rows, relayed_rows, p1, p2, t1, t2)
    pooled_pair = lax.ppermute(pooled, "wide", pair_swap(wide))
    pooled_far = lax.ppermute(pooled_pair, "wide", pair_relay_back(wide))
    mine = jnp.stack([pooled, pooled_pair, pooled_far])[None]
    bit = narrow // 2
    while bit > 1:
        other = lax.ppermute(mine, "narrow", pair_swap(narrow, bit))
        mine = jnp.stack([mine, other], axis=1).reshape((-1,) + mine.shape[1:])
        bit //= 2
    theirs = lax.ppermute(mine, "narrow", pair_swap(narrow))
    total = narrow * LANES
    coarse = pl.pallas_call(
        functools.partial(coarse_kernel, wide, narrow),
        out_shape=jax.ShapeDtypeStruct((o3, total), jnp.bfloat16),
        in_specs=[VMEM] * 3,
        out_specs=VMEM,
        scratch_shapes=[pltpu.VMEM((3 * c2, total), jnp.bfloat16)],
        compiler_params=params,
        cost_estimate=pl.CostEstimate(flops=10**9, bytes_accessed=10**6, transcendentals=0),
    )(mine, theirs, t3)
    return coarse[:, None, :]


def solution(mesh):
    in_specs = (P(None, "wide", "narrow", None), P(), P(), P(), P(), P("narrow", None))
    out_specs = P("narrow", "wide", None)
    return jax.shard_map(
        functools.partial(body, mesh.shape["wide"], mesh.shape["narrow"]),
        mesh=mesh,
        in_specs=in_specs,
        out_specs=out_specs,
        check_vma=False,
    )
```

```python
import functools

import jax
import jax.numpy as jnp
from jax import lax
from jax.experimental import pallas as pl
from jax.experimental.pallas import tpu as pltpu
from jax.sharding import PartitionSpec as P

LANES = 128
VMEM = pl.BlockSpec(memory_space=pltpu.VMEM)


def pair_swap(count, bit=1):
    return [(k, k ^ bit) for k in range(count)]


def pair_relay(count):
    steps = []
    for k in range(count):
        target = k - 2 if k % 2 == 0 else k + 2
        steps.append((k, target if 0 <= target < count else k ^ 1))
    return steps


def pair_relay_back(count):
    return [(target, source) for source, target in pair_relay(count)]


def weights_kernel(w1_ref, w2_ref, w3_ref, t1_ref, t2_ref, t3_ref):
    o1 = w1_ref.shape[0]
    c1 = w1_ref.shape[1] // 27
    o2 = w2_ref.shape[0]
    c2 = w2_ref.shape[1] // 27
    o3 = w3_ref.shape[0]
    c3 = w3_ref.shape[1] // 27
    for ref, out, o, c, rows in ((w1_ref, t1_ref, o1, c1, 4), (w2_ref, t2_ref, o2, c2, 2)):
        span = (rows + 2) * c
        for be in range(9):
            taps = [ref[:, (a * 9 + be) * c : (a * 9 + be + 1) * c] for a in range(3)]
            for row in range(rows):
                parts = []
                if row:
                    parts.append(jnp.zeros((o, row * c), jnp.bfloat16))
                parts += taps
                if row < rows - 1:
                    parts.append(jnp.zeros((o, (rows - 1 - row) * c), jnp.bfloat16))
                out[row * o : (row + 1) * o, be * span : (be + 1) * span] = jnp.concatenate(
                    parts, axis=1
                )
    for be in range(9):
        for a in range(3):
            t3_ref[be * o3 : (be + 1) * o3, a * c3 : (a + 1) * c3] = w3_ref[
                :, (a * 9 + be) * c3 : (a * 9 + be + 1) * c3
            ]


def shifted(value):
    lane = lax.broadcasted_iota(jnp.int32, value.shape, 1)
    low = jnp.where(lane == 0, 0.0, pltpu.roll(value, 1, 1))
    high = jnp.where(lane == LANES - 1, 0.0, pltpu.roll(value, LANES - 1, 1))
    return low, value, high


def column(row_ref):
    row = row_ref[...]
    square = (row.shape[1], row.shape[1])
    here = lax.broadcasted_iota(jnp.int32, square, 0) == lax.broadcasted_iota(jnp.int32, square, 1)
    return jnp.sum(jnp.where(here, jnp.broadcast_to(row, square), 0.0), axis=1, keepdims=True)


def unpack_kernel(raw_ref, scale_ref, shift_ref, out_ref, staged):
    c = scale_ref.shape[1]
    depth, height = out_ref.shape[0] // c, out_ref.shape[1] // LANES
    staged[...] = raw_ref[...].astype(jnp.float32)
    scale, shift = column(scale_ref), column(shift_ref)
    for d in range(depth):
        for h in range(height):
            rows = staged[pl.ds(d * height + h, c, stride=depth * height), :]
            out_ref[d * c : (d + 1) * c, h * LANES : (h + 1) * LANES] = (
                rows * scale + shift
            ).astype(jnp.bfloat16)


def slab_kernel(
    wide, raw_ref, scale_ref, shift_ref, own_ref, pair_ref, out_ref, relay_ref, side_ref, staged
):
    i, j = lax.axis_index("wide"), lax.axis_index("narrow")
    i_odd, j_odd = lax.rem(i, 2), lax.rem(j, 2)
    block, columns = own_ref.shape
    c = scale_ref.shape[1]
    depth, height = block // c, columns // LANES
    far_row = pl.multiple_of(2 * i_odd * block, block)
    pair_row = pl.multiple_of((2 - 2 * i_odd) * block, block)
    staged[...] = raw_ref[...].astype(jnp.float32)
    scale, shift = column(scale_ref), column(shift_ref)
    for d in range(depth):
        for h in range(height):
            rows = staged[pl.ds(d * height + h, c, stride=depth * height), :]
            out_ref[
                pl.ds(pl.multiple_of(far_row + d * c, c), c), h * LANES : (h + 1) * LANES
            ] = (rows * scale + shift).astype(jnp.bfloat16)

    @pl.when(jnp.where(i_odd == 0, i == 0, i == wide - 1))
    def _():
        out_ref[pl.ds(far_row, block), :] = jnp.zeros((block, columns), jnp.bfloat16)

    out_ref[block : 2 * block, :] = own_ref[...]
    out_ref[pl.ds(pair_row, block), :] = pair_ref[...]
    half = columns // 2
    relay_ref[...] = out_ref[:, pl.ds(pl.multiple_of(j_odd * half, half), half)]
    side_ref[...] = out_ref[:, pl.ds(pl.multiple_of((1 - j_odd) * half, half), half)]


def dot(a, b):
    return jnp.dot(a, b, preferred_element_type=jnp.float32)


def tile(ref, *picks):
    return jnp.concatenate([ref[:, k * LANES : (k + 1) * LANES] for k in picks], axis=1)


def spread(value, ref, at):
    rows, columns = value.shape
    for k in range(columns // LANES):
        parts = shifted(value[:, k * LANES : (k + 1) * LANES].astype(jnp.float32))
        for e, part in enumerate(parts):
            ref[e * rows : (e + 1) * rows, pl.ds(at + k * LANES, LANES)] = part.astype(jnp.bfloat16)


def clear_depth(wide, ref):
    i = lax.axis_index("wide")
    span = ref.shape[0] // 3
    c = span // 4

    @pl.when(i == 0)
    def _():
        for e in range(3):
            ref[e * span : e * span + c, :] = jnp.zeros((c, ref.shape[1]), jnp.bfloat16)

    @pl.when(i == wide - 1)
    def _():
        for e in range(3):
            ref[e * span + 3 * c : (e + 1) * span, :] = jnp.zeros((c, ref.shape[1]), jnp.bfloat16)


def thirds(ref):
    span = ref.shape[1] // 3
    return [ref[:, b * span : (b + 1) * span] for b in range(3)]


def centre_kernel(wide, x_ref, w1_ref, w2_ref, p1_ref, p2_ref, taps, hidden):
    spread(x_ref[...], taps, 0)
    first = thirds(w1_ref)
    columns = jnp.concatenate(
        [taps[:, b * LANES : (b + 2) * LANES] for b in range(3)], axis=0
    )
    spread(jnp.maximum(dot(w1_ref[...], columns), 0.0), hidden, 0)
    clear_depth(wide, hidden)
    r0 = dot(first[0], tile(taps, 2, 3))
    r1 = dot(first[1], tile(taps, 0, 3))
    r2 = dot(first[2], tile(taps, 0, 1))
    p1_ref[:, 0:LANES] = r2[:, :LANES]
    p1_ref[:, LANES : 2 * LANES] = r2[:, LANES:] + r1[:, :LANES]
    p1_ref[:, 2 * LANES : 3 * LANES] = r0[:, LANES:]
    p1_ref[:, 3 * LANES :] = r1[:, LANES:] + r0[:, :LANES]
    both = hidden[...]
    q0, q1, q2 = (dot(w, both) for w in thirds(w2_ref))
    p2_ref[:, 0:LANES] = q2[:, :LANES]
    p2_ref[:, LANES : 2 * LANES] = q2[:, LANES:] + q1[:, :LANES]
    p2_ref[:, 2 * LANES : 3 * LANES] = q0[:, LANES:]
    p2_ref[:, 3 * LANES :] = q1[:, LANES:] + q0[:, :LANES]


def side_terms(wide, narrow, high, last, rows_ref, p1_ref, w1_ref, w2_ref, taps, hidden):
    span1, span2 = w1_ref.shape[1] // 3, w2_ref.shape[1] // 3
    outer1, outer2 = pl.multiple_of(2 * high * span1, LANES), pl.multiple_of(2 * high * span2, LANES)
    for k in range(2):
        at = pl.multiple_of((k + high * (1 - 2 * k)) * LANES, LANES)
        spread(rows_ref[:, k * LANES : (k + 1) * LANES], taps, at)

    @pl.when(last)
    def _():
        taps[...] = jnp.zeros_like(taps)

    r = dot(w1_ref[:, pl.ds(outer1, span1)], taps[...])
    r1 = dot(w1_ref[:, span1 : 2 * span1], taps[:, LANES:])
    before = p1_ref[:, pl.ds(pl.multiple_of(high * 2 * LANES, LANES), 2 * LANES)]
    spread(jnp.maximum(r[:, :LANES] + r1 + before[:, :LANES], 0.0), hidden, 0)
    spread(jnp.maximum(r[:, LANES:] + before[:, LANES:], 0.0), hidden, LANES)
    clear_depth(wide, hidden)

    @pl.when(last)
    def _():
        hidden[:, :LANES] = jnp.zeros((hidden.shape[0], LANES), jnp.bfloat16)

    q = dot(w2_ref[:, pl.ds(outer2, span2)], hidden[...])
    q1 = dot(w2_ref[:, span2 : 2 * span2], hidden[:, LANES:])
    return q[:, :LANES] + q1, q[:, LANES:]


def partner_kernel(
    wide, narrow, rows_ref, p1_ref, p2_ref, w1_ref, w2_ref, out_ref, taps, hidden
):
    high = 1 - lax.rem(lax.axis_index("narrow"), 2)
    end, near = side_terms(
        wide, narrow, high, False, rows_ref, p1_ref, w1_ref, w2_ref, taps, hidden
    )
    at = pl.multiple_of(high * 2 * LANES, LANES)
    out_ref[...] = p2_ref[...]
    out_ref[:, pl.ds(at, LANES)] += end
    out_ref[:, pl.ds(at + LANES, LANES)] += near


def edge_kernel(
    wide, narrow, rows_ref, p1_ref, p2_ref, w1_ref, w2_ref, out_ref, taps, hidden
):
    j = lax.axis_index("narrow")
    high = lax.rem(j, 2)
    last = jnp.where(high == 0, j == 0, j == narrow - 1)
    end, near = side_terms(
        wide, narrow, high, last, rows_ref, p1_ref, w1_ref, w2_ref, taps, hidden
    )
    c2 = out_ref.shape[0]
    at = pl.multiple_of(high * 2 * LANES, LANES)
    other = pl.multiple_of((1 - high) * 2 * LANES, LANES)

    def best(one, two):
        value = jnp.maximum(one, two)
        value = jnp.maximum(jnp.maximum(value[:c2], value[c2:]), 0.0)
        return jnp.maximum(value, pltpu.roll(value, LANES - 1, 1)).astype(jnp.bfloat16)

    mine = best(end + p2_ref[:, pl.ds(at, LANES)], near + p2_ref[:, pl.ds(at + LANES, LANES)])
    rest = best(p2_ref[:, pl.ds(other, LANES)], p2_ref[:, pl.ds(other + LANES, LANES)])
    cell = lax.broadcasted_iota(jnp.int32, (2 * LANES, LANES), 0)
    target = lax.broadcasted_iota(jnp.int32, (2 * LANES, LANES), 1)
    wanted = jnp.bitwise_xor(2 * target, high * LANES)
    pick = (cell == wanted).astype(jnp.bfloat16)
    out_ref[...] = dot(jnp.concatenate([mine, rest], axis=1), pick).astype(jnp.bfloat16)


def coarse_products(wide, bit, blocks_ref, w3_ref, z_ref, slab):
    i, j = lax.axis_index("wide"), lax.axis_index("narrow")
    i_odd = lax.rem(i, 2)
    groups, _, c, lanes = blocks_ref.shape
    slots = (1, 2 - 2 * i_odd, 2 * i_odd)
    for r in range(groups):
        for k in range(3):
            slab[pl.ds(pl.multiple_of(slots[k] * c, c), c), r * lanes : (r + 1) * lanes] = blocks_ref[
                r, k
            ]

    @pl.when(i == 0)
    def _():
        slab[0:c, :] = jnp.zeros((c, slab.shape[1]), jnp.bfloat16)

    @pl.when(i == wide - 1)
    def _():
        slab[2 * c :, :] = jnp.zeros((c, slab.shape[1]), jnp.bfloat16)

    z = dot(w3_ref[...], slab[...])
    for r in range(groups):
        at = pl.multiple_of(jnp.bitwise_xor(j, 2 * r + bit) * lanes, lanes)
        z_ref[:, pl.ds(at, lanes)] = z[:, r * lanes : (r + 1) * lanes]


def coarse_first_kernel(wide, blocks_ref, w3_ref, z_ref, slab):
    coarse_products(wide, 0, blocks_ref, w3_ref, z_ref, slab)


def coarse_kernel(wide, blocks_ref, w3_ref, first_ref, out_ref, z_ref, slab):
    del first_ref
    coarse_products(wide, 1, blocks_ref, w3_ref, z_ref, slab)
    o, total = out_ref.shape
    width = LANES // 2
    count = total // LANES
    lane = lax.broadcasted_iota(jnp.int32, (o, LANES), 1)
    column_of = lax.rem(lane, width)

    def z(b, e, q):
        if q < 0 or q >= count:
            return jnp.zeros((o, LANES), jnp.float32)
        at = (b * 3 + e) * o
        return z_ref[at : at + o, q * LANES : (q + 1) * LANES]

    for q in range(count):
        terms = []
        for e in range(3):
            crossed = jnp.where(
                lane < width, z(0, e, q) + z(2, e, q + 1), z(0, e, q - 1) + z(2, e, q)
            )
            terms.append(z(1, e, q) + pltpu.roll(crossed, width, 1))
        low = jnp.where(column_of == 0, 0.0, pltpu.roll(terms[0], 1, 1))
        high = jnp.where(column_of == width - 1, 0.0, pltpu.roll(terms[2], LANES - 1, 1))
        out_ref[:, q * LANES : (q + 1) * LANES] = jnp.maximum(low + terms[1] + high, 0.0).astype(
            jnp.bfloat16
        )


def body(
    wide, narrow, stored_features, channel_scale, channel_shift, first_weight, second_weight,
    third_weight,
):
    c1, depth, height, width = stored_features.shape
    c2 = second_weight.shape[0]
    o3 = third_weight.shape[0]
    params = pltpu.CompilerParams(vmem_limit_bytes=24 * 1024 * 1024)
    rows = c1 * depth * height
    columns = height * width
    scale, shift = channel_scale.reshape(1, c1), channel_shift.reshape(1, c1)

    def cost(flops, size):
        return pl.CostEstimate(flops=flops, bytes_accessed=size, transcendentals=0)

    def unpack(block):
        return pl.pallas_call(
            unpack_kernel,
            out_shape=jax.ShapeDtypeStruct((depth * c1, columns), jnp.bfloat16),
            in_specs=[VMEM] * 3,
            out_specs=VMEM,
            scratch_shapes=[pltpu.VMEM((rows, width), jnp.float32)],
            compiler_params=params,
            cost_estimate=cost(10**6, 10**6),
        )(block.reshape(rows, width), scale, shift)

    pair = lax.ppermute(stored_features, "wide", pair_swap(wide))
    t1, t2, t3 = pl.pallas_call(
        weights_kernel,
        out_shape=(
            jax.ShapeDtypeStruct((4 * c1, 9 * 6 * c1), jnp.bfloat16),
            jax.ShapeDtypeStruct((2 * c2, 9 * 4 * c1), jnp.bfloat16),
            jax.ShapeDtypeStruct((9 * o3, 3 * c2), jnp.bfloat16),
        ),
        in_specs=[VMEM] * 3,
        out_specs=(VMEM,) * 3,
        compiler_params=params,
        cost_estimate=cost(10**6, 4 * 10**6),
    )(first_weight, second_weight, third_weight)
    own_slab = unpack(stored_features)
    pair, own_slab, t1, t2, t3 = lax.optimization_barrier((pair, own_slab, t1, t2, t3))
    far = lax.ppermute(pair, "wide", pair_relay_back(wide))
    pair_slab = unpack(pair)
    slab, relay, side = pl.pallas_call(
        functools.partial(slab_kernel, wide),
        out_shape=(
            jax.ShapeDtypeStruct((6 * c1, columns), jnp.bfloat16),
            jax.ShapeDtypeStruct((6 * c1, columns // 2), jnp.bfloat16),
            jax.ShapeDtypeStruct((6 * c1, columns // 2), jnp.bfloat16),
        ),
        in_specs=[VMEM] * 5,
        out_specs=(VMEM,) * 3,
        scratch_shapes=[pltpu.VMEM((rows, width), jnp.float32)],
        compiler_params=params,
        cost_estimate=cost(10**6, 2 * 10**6),
    )(far.reshape(rows, width), scale, shift, own_slab, pair_slab)
    passed = lax.ppermute(relay, "narrow", pair_relay(narrow))
    partner_rows = lax.ppermute(side, "narrow", pair_swap(narrow))
    p1, p2 = pl.pallas_call(
        functools.partial(centre_kernel, wide),
        out_shape=(
            jax.ShapeDtypeStruct((4 * c1, 4 * width), jnp.float32),
            jax.ShapeDtypeStruct((2 * c2, 4 * width), jnp.float32),
        ),
        in_specs=[VMEM] * 3,
        out_specs=(VMEM,) * 2,
        scratch_shapes=[
            pltpu.VMEM((18 * c1, 4 * width), jnp.bfloat16),
            pltpu.VMEM((12 * c1, 2 * width), jnp.bfloat16),
        ],
        compiler_params=params,
        cost_estimate=cost(2 * 10**9, 4 * 10**6),
    )(slab, t1, t2)
    passed, p1, p2 = lax.optimization_barrier((passed, p1, p2))
    relayed_rows = lax.ppermute(passed, "narrow", pair_swap(narrow))

    def side(kernel, out, rows, before):
        return pl.pallas_call(
            functools.partial(kernel, wide, narrow),
            out_shape=out,
            in_specs=[VMEM] * 5,
            out_specs=VMEM,
            scratch_shapes=[
                pltpu.VMEM((18 * c1, 2 * width), jnp.bfloat16),
                pltpu.VMEM((12 * c1, 2 * width), jnp.bfloat16),
            ],
            compiler_params=params,
            cost_estimate=cost(10**9, 4 * 10**6),
        )(rows, p1, before, t1, t2)

    p2 = side(partner_kernel, jax.ShapeDtypeStruct(p2.shape, p2.dtype), partner_rows, p2)
    pooled = side(edge_kernel, jax.ShapeDtypeStruct((c2, LANES), jnp.bfloat16), relayed_rows, p2)
    pooled_pair = lax.ppermute(pooled, "wide", pair_swap(wide))
    pooled_far = lax.ppermute(pooled_pair, "wide", pair_relay_back(wide))
    mine = jnp.stack([pooled, pooled_pair, pooled_far])[None]
    bit = narrow // 2
    while bit > 1:
        other = lax.ppermute(mine, "narrow", pair_swap(narrow, bit))
        mine = jnp.stack([mine, other], axis=1).reshape((-1,) + mine.shape[1:])
        bit //= 2
    theirs = lax.ppermute(mine, "narrow", pair_swap(narrow))
    total = narrow * LANES
    products = jax.ShapeDtypeStruct((9 * o3, total), jnp.float32)
    scratch = [pltpu.VMEM((3 * c2, total // 2), jnp.bfloat16)]
    first = pl.pallas_call(
        functools.partial(coarse_first_kernel, wide),
        out_shape=products,
        in_specs=[VMEM] * 2,
        out_specs=VMEM,
        scratch_shapes=scratch,
        compiler_params=params,
        cost_estimate=cost(10**9, 10**6),
    )(mine, t3)
    coarse, _ = pl.pallas_call(
        functools.partial(coarse_kernel, wide),
        out_shape=(jax.ShapeDtypeStruct((o3, total), jnp.bfloat16), products),
        in_specs=[VMEM] * 3,
        out_specs=(VMEM,) * 2,
        scratch_shapes=scratch,
        input_output_aliases={2: 1},
        compiler_params=params,
        cost_estimate=cost(10**9, 10**6),
    )(theirs, t3, first)
    return coarse[:, None, :]


def solution(mesh):
    in_specs = (P(None, "wide", "narrow", None), P(), P(), P(), P(), P("narrow", None))
    out_specs = P("narrow", "wide", None)
    return jax.shard_map(
        functools.partial(body, mesh.shape["wide"], mesh.shape["narrow"]),
        mesh=mesh,
        in_specs=in_specs,
        out_specs=out_specs,
        check_vma=False,
    )
```

```python
import functools

import jax
import jax.numpy as jnp
from jax import lax
from jax.experimental import pallas as pl
from jax.experimental.pallas import tpu as pltpu
from jax.sharding import PartitionSpec as P

LANES = 128
VMEM = pl.BlockSpec(memory_space=pltpu.VMEM)


def pair_swap(count, bit=1):
    return [(k, k ^ bit) for k in range(count)]


def pair_relay(count):
    steps = []
    for k in range(count):
        target = k - 2 if k % 2 == 0 else k + 2
        steps.append((k, target if 0 <= target < count else k ^ 1))
    return steps


def pair_relay_back(count):
    return [(target, source) for source, target in pair_relay(count)]


def weights_kernel(wide, w1_ref, w2_ref, w3_ref, t1_ref, t2_ref, t3_ref):
    i = lax.axis_index("wide")
    keep_low = jnp.where(i == 0, 0.0, 1.0)
    keep_high = jnp.where(i == wide - 1, 0.0, 1.0)

    def kept(value, keep):
        return (value.astype(jnp.float32) * keep).astype(jnp.bfloat16)

    o1 = w1_ref.shape[0]
    c1 = w1_ref.shape[1] // 27
    o2 = w2_ref.shape[0]
    c2 = w2_ref.shape[1] // 27
    o3 = w3_ref.shape[0]
    c3 = w3_ref.shape[1] // 27
    for ref, out, o, c, rows in ((w1_ref, t1_ref, o1, c1, 4), (w2_ref, t2_ref, o2, c2, 2)):
        span = (rows + 2) * c
        for be in range(9):
            taps = [ref[:, (a * 9 + be) * c : (a * 9 + be + 1) * c] for a in range(3)]
            for row in range(rows):
                parts = []
                if row:
                    parts.append(jnp.zeros((o, row * c), jnp.bfloat16))
                parts += taps
                if row < rows - 1:
                    parts.append(jnp.zeros((o, (rows - 1 - row) * c), jnp.bfloat16))
                value = jnp.concatenate(parts, axis=1)
                if rows == 4 and row in (0, 3):
                    value = kept(value, keep_low if row == 0 else keep_high)
                out[row * o : (row + 1) * o, be * span : (be + 1) * span] = value
    for be in range(9):
        for a in range(3):
            value = w3_ref[:, (a * 9 + be) * c3 : (a * 9 + be + 1) * c3]
            if a != 1:
                value = kept(value, keep_low if a == 0 else keep_high)
            t3_ref[be * o3 : (be + 1) * o3, a * c3 : (a + 1) * c3] = value


def shifted(value):
    lane = lax.broadcasted_iota(jnp.int32, value.shape, 1)
    low = jnp.where(lane == 0, 0.0, pltpu.roll(value, 1, 1))
    high = jnp.where(lane == LANES - 1, 0.0, pltpu.roll(value, LANES - 1, 1))
    return low, value, high


def column(row_ref):
    row = row_ref[...]
    square = (row.shape[1], row.shape[1])
    here = lax.broadcasted_iota(jnp.int32, square, 0) == lax.broadcasted_iota(jnp.int32, square, 1)
    return jnp.sum(jnp.where(here, jnp.broadcast_to(row, square), 0.0), axis=1, keepdims=True)


def unpack_kernel(raw_ref, scale_ref, shift_ref, out_ref, staged):
    c = scale_ref.shape[1]
    depth, height = out_ref.shape[0] // c, out_ref.shape[1] // LANES
    staged[...] = raw_ref[...].astype(jnp.float32)
    scale, shift = column(scale_ref), column(shift_ref)
    for d in range(depth):
        for h in range(height):
            rows = staged[pl.ds(d * height + h, c, stride=depth * height), :]
            out_ref[d * c : (d + 1) * c, h * LANES : (h + 1) * LANES] = (
                rows * scale + shift
            ).astype(jnp.bfloat16)


def slab_kernel(
    wide, raw_ref, scale_ref, shift_ref, own_ref, pair_ref, out_ref, relay_ref, side_ref, staged
):
    i, j = lax.axis_index("wide"), lax.axis_index("narrow")
    i_odd, j_odd = lax.rem(i, 2), lax.rem(j, 2)
    block, columns = own_ref.shape
    c = scale_ref.shape[1]
    depth, height = block // c, columns // LANES
    far_row = pl.multiple_of(2 * i_odd * block, block)
    pair_row = pl.multiple_of((2 - 2 * i_odd) * block, block)
    keep = jnp.where(i == i_odd * (wide - 1), 0.0, 1.0)
    staged[...] = raw_ref[...].astype(jnp.float32)
    scale, shift = column(scale_ref) * keep, column(shift_ref) * keep
    for d in range(depth):
        for h in range(height):
            rows = staged[pl.ds(d * height + h, c, stride=depth * height), :]
            out_ref[
                pl.ds(pl.multiple_of(far_row + d * c, c), c), h * LANES : (h + 1) * LANES
            ] = (rows * scale + shift).astype(jnp.bfloat16)
    out_ref[block : 2 * block, :] = own_ref[...]
    out_ref[pl.ds(pair_row, block), :] = pair_ref[...]
    half = columns // 2
    relay_ref[...] = out_ref[:, pl.ds(pl.multiple_of(j_odd * half, half), half)]
    side_ref[...] = out_ref[:, pl.ds(pl.multiple_of((1 - j_odd) * half, half), half)]


def dot(a, b):
    return jnp.dot(a, b, preferred_element_type=jnp.float32)


def tile(ref, *picks):
    return jnp.concatenate([ref[:, k * LANES : (k + 1) * LANES] for k in picks], axis=1)


def spread(value, ref, at):
    rows, columns = value.shape
    for k in range(columns // LANES):
        parts = shifted(value[:, k * LANES : (k + 1) * LANES].astype(jnp.float32))
        for e, part in enumerate(parts):
            ref[e * rows : (e + 1) * rows, pl.ds(at + k * LANES, LANES)] = part.astype(jnp.bfloat16)


def thirds(ref):
    span = ref.shape[1] // 3
    return [ref[:, b * span : (b + 1) * span] for b in range(3)]


def centre_kernel(x_ref, w1_ref, p1_ref, hidden_ref, taps):
    spread(x_ref[...], taps, 0)
    first = thirds(w1_ref)
    columns = jnp.concatenate(
        [taps[:, b * LANES : (b + 2) * LANES] for b in range(3)], axis=0
    )
    spread(jnp.maximum(dot(w1_ref[...], columns), 0.0), hidden_ref, 0)
    r0 = dot(first[0], tile(taps, 2, 3))
    r1 = dot(first[1], tile(taps, 0, 3))
    r2 = dot(first[2], tile(taps, 0, 1))
    p1_ref[:, 0:LANES] = r2[:, :LANES]
    p1_ref[:, LANES : 2 * LANES] = r2[:, LANES:] + r1[:, :LANES]
    p1_ref[:, 2 * LANES : 3 * LANES] = r0[:, LANES:]
    p1_ref[:, 3 * LANES :] = r1[:, LANES:] + r0[:, :LANES]


def second_kernel(hidden_ref, w2_ref, p2_ref):
    both = hidden_ref[...]
    q0, q1, q2 = (dot(w, both) for w in thirds(w2_ref))
    p2_ref[:, 0:LANES] = q2[:, :LANES]
    p2_ref[:, LANES : 2 * LANES] = q2[:, LANES:] + q1[:, :LANES]
    p2_ref[:, 2 * LANES : 3 * LANES] = q0[:, LANES:]
    p2_ref[:, 3 * LANES :] = q1[:, LANES:] + q0[:, :LANES]


def side_terms(high, keep, rows_ref, p1_ref, w1_ref, w2_ref, taps, hidden):
    span1, span2 = w1_ref.shape[1] // 3, w2_ref.shape[1] // 3
    outer1, outer2 = pl.multiple_of(2 * high * span1, LANES), pl.multiple_of(2 * high * span2, LANES)
    for k in range(2):
        at = pl.multiple_of((k + high * (1 - 2 * k)) * LANES, LANES)
        value = rows_ref[:, k * LANES : (k + 1) * LANES].astype(jnp.float32)
        spread(value if keep is None else value * keep, taps, at)
    r = dot(w1_ref[:, pl.ds(outer1, span1)], taps[...])
    r1 = dot(w1_ref[:, span1 : 2 * span1], taps[:, LANES:])
    before = p1_ref[:, pl.ds(pl.multiple_of(high * 2 * LANES, LANES), 2 * LANES)]
    end = jnp.maximum(r[:, :LANES] + r1 + before[:, :LANES], 0.0)
    spread(end if keep is None else end * keep, hidden, 0)
    spread(jnp.maximum(r[:, LANES:] + before[:, LANES:], 0.0), hidden, LANES)
    q = dot(w2_ref[:, pl.ds(outer2, span2)], hidden[...])
    q1 = dot(w2_ref[:, span2 : 2 * span2], hidden[:, LANES:])
    return q[:, :LANES] + q1, q[:, LANES:]


def partner_kernel(narrow, rows_ref, p1_ref, p2_ref, w1_ref, w2_ref, out_ref, taps, hidden):
    high = 1 - lax.rem(lax.axis_index("narrow"), 2)
    end, near = side_terms(high, None, rows_ref, p1_ref, w1_ref, w2_ref, taps, hidden)
    at = pl.multiple_of(high * 2 * LANES, LANES)
    out_ref[...] = p2_ref[...]
    out_ref[:, pl.ds(at, LANES)] += end
    out_ref[:, pl.ds(at + LANES, LANES)] += near


def edge_kernel(narrow, rows_ref, p1_ref, p2_ref, w1_ref, w2_ref, out_ref, taps, hidden):
    j = lax.axis_index("narrow")
    high = lax.rem(j, 2)
    keep = jnp.where(j == high * (narrow - 1), 0.0, 1.0)
    end, near = side_terms(high, keep, rows_ref, p1_ref, w1_ref, w2_ref, taps, hidden)
    c2 = out_ref.shape[0]
    at = pl.multiple_of(high * 2 * LANES, LANES)
    other = pl.multiple_of((1 - high) * 2 * LANES, LANES)

    def best(one, two):
        value = jnp.maximum(one, two)
        value = jnp.maximum(jnp.maximum(value[:c2], value[c2:]), 0.0)
        return jnp.maximum(value, pltpu.roll(value, LANES - 1, 1)).astype(jnp.bfloat16)

    mine = best(end + p2_ref[:, pl.ds(at, LANES)], near + p2_ref[:, pl.ds(at + LANES, LANES)])
    rest = best(p2_ref[:, pl.ds(other, LANES)], p2_ref[:, pl.ds(other + LANES, LANES)])
    cell = lax.broadcasted_iota(jnp.int32, (2 * LANES, LANES), 0)
    target = lax.broadcasted_iota(jnp.int32, (2 * LANES, LANES), 1)
    wanted = jnp.bitwise_xor(2 * target, high * LANES)
    pick = (cell == wanted).astype(jnp.bfloat16)
    out_ref[...] = dot(jnp.concatenate([mine, rest], axis=1), pick).astype(jnp.bfloat16)


def coarse_products(bit, blocks_ref, w3_ref, z_ref, slab):
    i, j = lax.axis_index("wide"), lax.axis_index("narrow")
    i_odd = lax.rem(i, 2)
    groups, _, c, lanes = blocks_ref.shape
    slots = (1, 2 - 2 * i_odd, 2 * i_odd)
    for r in range(groups):
        for k in range(3):
            slab[pl.ds(pl.multiple_of(slots[k] * c, c), c), r * lanes : (r + 1) * lanes] = blocks_ref[
                r, k
            ]

    z = dot(w3_ref[...], slab[...])
    for r in range(groups):
        at = pl.multiple_of(jnp.bitwise_xor(j, 2 * r + bit) * lanes, lanes)
        z_ref[:, pl.ds(at, lanes)] = z[:, r * lanes : (r + 1) * lanes]


def coarse_first_kernel(blocks_ref, w3_ref, z_ref, slab):
    coarse_products(0, blocks_ref, w3_ref, z_ref, slab)


def coarse_kernel(blocks_ref, w3_ref, first_ref, out_ref, z_ref, slab):
    del first_ref
    coarse_products(1, blocks_ref, w3_ref, z_ref, slab)
    o, total = out_ref.shape
    width = LANES // 2
    count = total // LANES
    lane = lax.broadcasted_iota(jnp.int32, (o, LANES), 1)
    column_of = lax.rem(lane, width)

    def z(b, e, q):
        if q < 0 or q >= count:
            return jnp.zeros((o, LANES), jnp.float32)
        at = (b * 3 + e) * o
        return z_ref[at : at + o, q * LANES : (q + 1) * LANES]

    for q in range(count):
        terms = []
        for e in range(3):
            crossed = jnp.where(
                lane < width, z(0, e, q) + z(2, e, q + 1), z(0, e, q - 1) + z(2, e, q)
            )
            terms.append(z(1, e, q) + pltpu.roll(crossed, width, 1))
        low = jnp.where(column_of == 0, 0.0, pltpu.roll(terms[0], 1, 1))
        high = jnp.where(column_of == width - 1, 0.0, pltpu.roll(terms[2], LANES - 1, 1))
        out_ref[:, q * LANES : (q + 1) * LANES] = jnp.maximum(low + terms[1] + high, 0.0).astype(
            jnp.bfloat16
        )


def body(
    wide, narrow, stored_features, channel_scale, channel_shift, first_weight, second_weight,
    third_weight,
):
    c1, depth, height, width = stored_features.shape
    c2 = second_weight.shape[0]
    o3 = third_weight.shape[0]
    params = pltpu.CompilerParams(vmem_limit_bytes=24 * 1024 * 1024)
    rows = c1 * depth * height
    columns = height * width
    scale, shift = channel_scale.reshape(1, c1), channel_shift.reshape(1, c1)

    def cost(flops, size):
        return pl.CostEstimate(flops=flops, bytes_accessed=size, transcendentals=0)

    def unpack(block):
        return pl.pallas_call(
            unpack_kernel,
            out_shape=jax.ShapeDtypeStruct((depth * c1, columns), jnp.bfloat16),
            in_specs=[VMEM] * 3,
            out_specs=VMEM,
            scratch_shapes=[pltpu.VMEM((rows, width), jnp.float32)],
            compiler_params=params,
            cost_estimate=cost(10**6, 10**6),
        )(block.reshape(rows, width), scale, shift)

    pair = lax.ppermute(stored_features, "wide", pair_swap(wide))
    t1, t2, t3 = pl.pallas_call(
        functools.partial(weights_kernel, wide),
        out_shape=(
            jax.ShapeDtypeStruct((4 * c1, 9 * 6 * c1), jnp.bfloat16),
            jax.ShapeDtypeStruct((2 * c2, 9 * 4 * c1), jnp.bfloat16),
            jax.ShapeDtypeStruct((9 * o3, 3 * c2), jnp.bfloat16),
        ),
        in_specs=[VMEM] * 3,
        out_specs=(VMEM,) * 3,
        compiler_params=params,
        cost_estimate=cost(10**6, 4 * 10**6),
    )(first_weight, second_weight, third_weight)
    pair, t1, t2, t3 = lax.optimization_barrier((pair, t1, t2, t3))
    own_slab = unpack(stored_features)
    far = lax.ppermute(pair, "wide", pair_relay_back(wide))
    pair_slab = unpack(pair)
    slab, relay, side = pl.pallas_call(
        functools.partial(slab_kernel, wide),
        out_shape=(
            jax.ShapeDtypeStruct((6 * c1, columns), jnp.bfloat16),
            jax.ShapeDtypeStruct((6 * c1, columns // 2), jnp.bfloat16),
            jax.ShapeDtypeStruct((6 * c1, columns // 2), jnp.bfloat16),
        ),
        in_specs=[VMEM] * 5,
        out_specs=(VMEM,) * 3,
        scratch_shapes=[pltpu.VMEM((rows, width), jnp.float32)],
        compiler_params=params,
        cost_estimate=cost(10**6, 2 * 10**6),
    )(far.reshape(rows, width), scale, shift, own_slab, pair_slab)
    passed = lax.ppermute(relay, "narrow", pair_relay(narrow))
    p1, hidden = pl.pallas_call(
        centre_kernel,
        out_shape=(
            jax.ShapeDtypeStruct((4 * c1, 4 * width), jnp.float32),
            jax.ShapeDtypeStruct((12 * c1, 2 * width), jnp.bfloat16),
        ),
        in_specs=[VMEM] * 2,
        out_specs=(VMEM,) * 2,
        scratch_shapes=[pltpu.VMEM((18 * c1, 4 * width), jnp.bfloat16)],
        compiler_params=params,
        cost_estimate=cost(2 * 10**9, 4 * 10**6),
    )(slab, t1)
    side, p1, hidden = lax.optimization_barrier((side, p1, hidden))
    partner_rows = lax.ppermute(side, "narrow", pair_swap(narrow))
    p2 = pl.pallas_call(
        second_kernel,
        out_shape=jax.ShapeDtypeStruct((2 * c2, 4 * width), jnp.float32),
        in_specs=[VMEM] * 2,
        out_specs=VMEM,
        compiler_params=params,
        cost_estimate=cost(10**9, 2 * 10**6),
    )(hidden, t2)
    passed, p1, p2 = lax.optimization_barrier((passed, p1, p2))
    relayed_rows = lax.ppermute(passed, "narrow", pair_swap(narrow))

    def add_side(kernel, out, rows, before):
        return pl.pallas_call(
            functools.partial(kernel, narrow),
            out_shape=out,
            in_specs=[VMEM] * 5,
            out_specs=VMEM,
            scratch_shapes=[
                pltpu.VMEM((18 * c1, 2 * width), jnp.bfloat16),
                pltpu.VMEM((12 * c1, 2 * width), jnp.bfloat16),
            ],
            compiler_params=params,
            cost_estimate=cost(10**9, 4 * 10**6),
        )(rows, p1, before, t1, t2)

    p2 = add_side(partner_kernel, jax.ShapeDtypeStruct(p2.shape, p2.dtype), partner_rows, p2)
    pooled = add_side(edge_kernel, jax.ShapeDtypeStruct((c2, LANES), jnp.bfloat16), relayed_rows, p2)
    pooled_pair = lax.ppermute(pooled, "wide", pair_swap(wide))
    pooled_far = lax.ppermute(pooled_pair, "wide", pair_relay_back(wide))
    mine = jnp.stack([pooled, pooled_pair, pooled_far])[None]
    bit = narrow // 2
    while bit > 1:
        other = lax.ppermute(mine, "narrow", pair_swap(narrow, bit))
        mine = jnp.stack([mine, other], axis=1).reshape((-1,) + mine.shape[1:])
        bit //= 2
    theirs = lax.ppermute(mine, "narrow", pair_swap(narrow))
    total = narrow * LANES
    products = jax.ShapeDtypeStruct((9 * o3, total), jnp.float32)
    scratch = [pltpu.VMEM((3 * c2, total // 2), jnp.bfloat16)]
    first = pl.pallas_call(
        coarse_first_kernel,
        out_shape=products,
        in_specs=[VMEM] * 2,
        out_specs=VMEM,
        scratch_shapes=scratch,
        compiler_params=params,
        cost_estimate=cost(10**9, 10**6),
    )(mine, t3)
    coarse, _ = pl.pallas_call(
        coarse_kernel,
        out_shape=(jax.ShapeDtypeStruct((o3, total), jnp.bfloat16), products),
        in_specs=[VMEM] * 3,
        out_specs=(VMEM,) * 2,
        scratch_shapes=scratch,
        input_output_aliases={2: 1},
        compiler_params=params,
        cost_estimate=cost(10**9, 10**6),
    )(theirs, t3, first)
    return coarse[:, None, :]


def solution(mesh):
    in_specs = (P(None, "wide", "narrow", None), P(), P(), P(), P(), P("narrow", None))
    out_specs = P("narrow", "wide", None)
    return jax.shard_map(
        functools.partial(body, mesh.shape["wide"], mesh.shape["narrow"]),
        mesh=mesh,
        in_specs=in_specs,
        out_specs=out_specs,
        check_vma=False,
    )
```

```python
import functools

import jax
import jax.numpy as jnp
from jax import lax
from jax.experimental import pallas as pl
from jax.experimental.pallas import tpu as pltpu
from jax.sharding import PartitionSpec as P

LANES = 128
VMEM = pl.BlockSpec(memory_space=pltpu.VMEM)


def pair_swap(count, bit=1):
    return [(k, k ^ bit) for k in range(count)]


BOTH = ("wide", "narrow")


def crossing(position, count):
    target = position + 1 if position % 2 else position - 1
    return target if 0 <= target < count else None


def cross_wide(wide, narrow):
    bit = 2 if narrow % 4 == 0 else 1
    steps = []
    for i in range(wide):
        for j in range(narrow):
            target = crossing(i, wide)
            end = i * narrow + (j ^ bit) if target is None else target * narrow + j
            steps.append((i * narrow + j, end))
    return steps


def cross_narrow(wide, narrow):
    steps = []
    for i in range(wide):
        for j in range(narrow):
            target = crossing(j, narrow)
            end = (i ^ 1) * narrow + j if target is None else i * narrow + target
            steps.append((i * narrow + j, end))
    return steps


def weights_kernel(wide, w1_ref, w2_ref, w3_ref, t1_ref, t2_ref, t3_ref):
    i = lax.axis_index("wide")
    keep_low = jnp.where(i == 0, 0.0, 1.0)
    keep_high = jnp.where(i == wide - 1, 0.0, 1.0)

    def kept(value, keep):
        return (value.astype(jnp.float32) * keep).astype(jnp.bfloat16)

    o1 = w1_ref.shape[0]
    c1 = w1_ref.shape[1] // 27
    o2 = w2_ref.shape[0]
    c2 = w2_ref.shape[1] // 27
    o3 = w3_ref.shape[0]
    c3 = w3_ref.shape[1] // 27
    for ref, out, o, c, rows in ((w1_ref, t1_ref, o1, c1, 4), (w2_ref, t2_ref, o2, c2, 2)):
        span = (rows + 2) * c
        for be in range(9):
            taps = [ref[:, (a * 9 + be) * c : (a * 9 + be + 1) * c] for a in range(3)]
            for row in range(rows):
                parts = []
                if row:
                    parts.append(jnp.zeros((o, row * c), jnp.bfloat16))
                parts += taps
                if row < rows - 1:
                    parts.append(jnp.zeros((o, (rows - 1 - row) * c), jnp.bfloat16))
                value = jnp.concatenate(parts, axis=1)
                if rows == 4 and row in (0, 3):
                    value = kept(value, keep_low if row == 0 else keep_high)
                out[row * o : (row + 1) * o, be * span : (be + 1) * span] = value
    for be in range(9):
        for a in range(3):
            value = w3_ref[:, (a * 9 + be) * c3 : (a * 9 + be + 1) * c3]
            if a != 1:
                value = kept(value, keep_low if a == 0 else keep_high)
            t3_ref[be * o3 : (be + 1) * o3, a * c3 : (a + 1) * c3] = value


def shifted(value):
    lane = lax.broadcasted_iota(jnp.int32, value.shape, 1)
    low = jnp.where(lane == 0, 0.0, pltpu.roll(value, 1, 1))
    high = jnp.where(lane == LANES - 1, 0.0, pltpu.roll(value, LANES - 1, 1))
    return low, value, high


def column(row_ref):
    row = row_ref[...]
    square = (row.shape[1], row.shape[1])
    here = lax.broadcasted_iota(jnp.int32, square, 0) == lax.broadcasted_iota(jnp.int32, square, 1)
    return jnp.sum(jnp.where(here, jnp.broadcast_to(row, square), 0.0), axis=1, keepdims=True)


def unpack_kernel(raw_ref, scale_ref, shift_ref, out_ref, staged):
    c = scale_ref.shape[1]
    depth, height = out_ref.shape[0] // c, out_ref.shape[1] // LANES
    staged[...] = raw_ref[...].astype(jnp.float32)
    scale, shift = column(scale_ref), column(shift_ref)
    for d in range(depth):
        for h in range(height):
            rows = staged[pl.ds(d * height + h, c, stride=depth * height), :]
            out_ref[d * c : (d + 1) * c, h * LANES : (h + 1) * LANES] = (
                rows * scale + shift
            ).astype(jnp.bfloat16)


def slab_kernel(
    wide, raw_ref, scale_ref, shift_ref, own_ref, pair_ref, out_ref, relay_ref, side_ref, staged
):
    i, j = lax.axis_index("wide"), lax.axis_index("narrow")
    i_odd, j_odd = lax.rem(i, 2), lax.rem(j, 2)
    block, columns = own_ref.shape
    c = scale_ref.shape[1]
    depth, height = block // c, columns // LANES
    far_row = pl.multiple_of(2 * i_odd * block, block)
    pair_row = pl.multiple_of((2 - 2 * i_odd) * block, block)
    keep = jnp.where(i == i_odd * (wide - 1), 0.0, 1.0)
    staged[...] = raw_ref[...].astype(jnp.float32)
    scale, shift = column(scale_ref) * keep, column(shift_ref) * keep
    for d in range(depth):
        for h in range(height):
            rows = staged[pl.ds(d * height + h, c, stride=depth * height), :]
            out_ref[
                pl.ds(pl.multiple_of(far_row + d * c, c), c), h * LANES : (h + 1) * LANES
            ] = (rows * scale + shift).astype(jnp.bfloat16)
    out_ref[block : 2 * block, :] = own_ref[...]
    out_ref[pl.ds(pair_row, block), :] = pair_ref[...]
    half = columns // 2
    relay_ref[...] = out_ref[:, pl.ds(pl.multiple_of(j_odd * half, half), half)]
    side_ref[...] = out_ref[:, pl.ds(pl.multiple_of((1 - j_odd) * half, half), half)]


def dot(a, b):
    return jnp.dot(a, b, preferred_element_type=jnp.float32)


def tile(ref, *picks):
    return jnp.concatenate([ref[:, k * LANES : (k + 1) * LANES] for k in picks], axis=1)


def spread(value, ref, at):
    rows, columns = value.shape
    for k in range(columns // LANES):
        parts = shifted(value[:, k * LANES : (k + 1) * LANES].astype(jnp.float32))
        for e, part in enumerate(parts):
            ref[e * rows : (e + 1) * rows, pl.ds(at + k * LANES, LANES)] = part.astype(jnp.bfloat16)


def thirds(ref):
    span = ref.shape[1] // 3
    return [ref[:, b * span : (b + 1) * span] for b in range(3)]


def centre_kernel(x_ref, w1_ref, p1_ref, hidden_ref, taps):
    spread(x_ref[...], taps, 0)
    first = thirds(w1_ref)
    columns = jnp.concatenate(
        [taps[:, b * LANES : (b + 2) * LANES] for b in range(3)], axis=0
    )
    spread(jnp.maximum(dot(w1_ref[...], columns), 0.0), hidden_ref, 0)
    r0 = dot(first[0], tile(taps, 2, 3))
    r1 = dot(first[1], tile(taps, 0, 3))
    r2 = dot(first[2], tile(taps, 0, 1))
    p1_ref[:, 0:LANES] = r2[:, :LANES]
    p1_ref[:, LANES : 2 * LANES] = r2[:, LANES:] + r1[:, :LANES]
    p1_ref[:, 2 * LANES : 3 * LANES] = r0[:, LANES:]
    p1_ref[:, 3 * LANES :] = r1[:, LANES:] + r0[:, :LANES]


def second_kernel(hidden_ref, w2_ref, p2_ref):
    both = hidden_ref[...]
    q0, q1, q2 = (dot(w, both) for w in thirds(w2_ref))
    p2_ref[:, 0:LANES] = q2[:, :LANES]
    p2_ref[:, LANES : 2 * LANES] = q2[:, LANES:] + q1[:, :LANES]
    p2_ref[:, 2 * LANES : 3 * LANES] = q0[:, LANES:]
    p2_ref[:, 3 * LANES :] = q1[:, LANES:] + q0[:, :LANES]


def side_terms(high, keep, rows_ref, p1_ref, w1_ref, w2_ref, taps, hidden):
    span1, span2 = w1_ref.shape[1] // 3, w2_ref.shape[1] // 3
    outer1, outer2 = pl.multiple_of(2 * high * span1, LANES), pl.multiple_of(2 * high * span2, LANES)
    for k in range(2):
        at = pl.multiple_of((k + high * (1 - 2 * k)) * LANES, LANES)
        value = rows_ref[:, k * LANES : (k + 1) * LANES].astype(jnp.float32)
        spread(value if keep is None else value * keep, taps, at)
    r = dot(w1_ref[:, pl.ds(outer1, span1)], taps[...])
    r1 = dot(w1_ref[:, span1 : 2 * span1], taps[:, LANES:])
    before = p1_ref[:, pl.ds(pl.multiple_of(high * 2 * LANES, LANES), 2 * LANES)]
    end = jnp.maximum(r[:, :LANES] + r1 + before[:, :LANES], 0.0)
    spread(end if keep is None else end * keep, hidden, 0)
    spread(jnp.maximum(r[:, LANES:] + before[:, LANES:], 0.0), hidden, LANES)
    q = dot(w2_ref[:, pl.ds(outer2, span2)], hidden[...])
    q1 = dot(w2_ref[:, span2 : 2 * span2], hidden[:, LANES:])
    return q[:, :LANES] + q1, q[:, LANES:]


def partner_kernel(narrow, rows_ref, p1_ref, p2_ref, w1_ref, w2_ref, out_ref, taps, hidden):
    high = 1 - lax.rem(lax.axis_index("narrow"), 2)
    end, near = side_terms(high, None, rows_ref, p1_ref, w1_ref, w2_ref, taps, hidden)
    at = pl.multiple_of(high * 2 * LANES, LANES)
    out_ref[...] = p2_ref[...]
    out_ref[:, pl.ds(at, LANES)] += end
    out_ref[:, pl.ds(at + LANES, LANES)] += near


def edge_kernel(narrow, rows_ref, p1_ref, p2_ref, w1_ref, w2_ref, out_ref, taps, hidden):
    j = lax.axis_index("narrow")
    high = lax.rem(j, 2)
    keep = jnp.where(j == high * (narrow - 1), 0.0, 1.0)
    end, near = side_terms(high, keep, rows_ref, p1_ref, w1_ref, w2_ref, taps, hidden)
    c2 = out_ref.shape[0]
    at = pl.multiple_of(high * 2 * LANES, LANES)
    other = pl.multiple_of((1 - high) * 2 * LANES, LANES)

    def best(one, two):
        value = jnp.maximum(one, two)
        value = jnp.maximum(jnp.maximum(value[:c2], value[c2:]), 0.0)
        return jnp.maximum(value, pltpu.roll(value, LANES - 1, 1)).astype(jnp.bfloat16)

    mine = best(end + p2_ref[:, pl.ds(at, LANES)], near + p2_ref[:, pl.ds(at + LANES, LANES)])
    rest = best(p2_ref[:, pl.ds(other, LANES)], p2_ref[:, pl.ds(other + LANES, LANES)])
    cell = lax.broadcasted_iota(jnp.int32, (2 * LANES, LANES), 0)
    target = lax.broadcasted_iota(jnp.int32, (2 * LANES, LANES), 1)
    wanted = jnp.bitwise_xor(2 * target, high * LANES)
    pick = (cell == wanted).astype(jnp.bfloat16)
    out_ref[...] = dot(jnp.concatenate([mine, rest], axis=1), pick).astype(jnp.bfloat16)


def coarse_products(places, blocks, w3_ref, z_ref, slab):
    i, j = lax.axis_index("wide"), lax.axis_index("narrow")
    i_odd = lax.rem(i, 2)
    slots = (1, 2 - 2 * i_odd, 2 * i_odd)
    at = 0
    for ref in blocks:
        for r in range(ref.shape[0]):
            for k in range(3):
                row = pl.multiple_of(slots[k] * ref.shape[2], ref.shape[2])
                slab[pl.ds(row, ref.shape[2]), at : at + LANES] = ref[r, k]
            at += LANES
    z = dot(w3_ref[...], slab[...])
    for k, place in enumerate(places):
        lane = pl.multiple_of(jnp.bitwise_xor(j, place) * LANES, LANES)
        z_ref[:, pl.ds(lane, LANES)] = z[:, k * LANES : (k + 1) * LANES]


def first_products_kernel(places, *refs):
    *blocks, w3_ref, z_ref, slab = refs
    coarse_products(places, blocks, w3_ref, z_ref, slab)


def more_products_kernel(places, *refs):
    *blocks, w3_ref, _, z_ref, slab = refs
    coarse_products(places, blocks, w3_ref, z_ref, slab)


def coarse_kernel(places, blocks_ref, w3_ref, before_ref, out_ref, z_ref, slab):
    del before_ref
    coarse_products(places, [blocks_ref], w3_ref, z_ref, slab)
    o, total = out_ref.shape
    width = LANES // 2
    count = total // LANES
    lane = lax.broadcasted_iota(jnp.int32, (o, LANES), 1)
    column_of = lax.rem(lane, width)

    def z(b, e, q):
        if q < 0 or q >= count:
            return jnp.zeros((o, LANES), jnp.float32)
        at = (b * 3 + e) * o
        return z_ref[at : at + o, q * LANES : (q + 1) * LANES]

    for q in range(count):
        terms = []
        for e in range(3):
            crossed = jnp.where(
                lane < width, z(0, e, q) + z(2, e, q + 1), z(0, e, q - 1) + z(2, e, q)
            )
            terms.append(z(1, e, q) + pltpu.roll(crossed, width, 1))
        low = jnp.where(column_of == 0, 0.0, pltpu.roll(terms[0], 1, 1))
        high = jnp.where(column_of == width - 1, 0.0, pltpu.roll(terms[2], LANES - 1, 1))
        out_ref[:, q * LANES : (q + 1) * LANES] = jnp.maximum(low + terms[1] + high, 0.0).astype(
            jnp.bfloat16
        )


def body(
    wide, narrow, stored_features, channel_scale, channel_shift, first_weight, second_weight,
    third_weight,
):
    c1, depth, height, width = stored_features.shape
    c2 = second_weight.shape[0]
    o3 = third_weight.shape[0]
    params = pltpu.CompilerParams(vmem_limit_bytes=24 * 1024 * 1024)
    rows = c1 * depth * height
    columns = height * width
    scale, shift = channel_scale.reshape(1, c1), channel_shift.reshape(1, c1)

    def cost(flops, size):
        return pl.CostEstimate(flops=flops, bytes_accessed=size, transcendentals=0)

    def unpack(block):
        return pl.pallas_call(
            unpack_kernel,
            out_shape=jax.ShapeDtypeStruct((depth * c1, columns), jnp.bfloat16),
            in_specs=[VMEM] * 3,
            out_specs=VMEM,
            scratch_shapes=[pltpu.VMEM((rows, width), jnp.float32)],
            compiler_params=params,
            cost_estimate=cost(10**6, 10**6),
        )(block.reshape(rows, width), scale, shift)

    far = lax.ppermute(stored_features, BOTH, cross_wide(wide, narrow))
    pair = lax.ppermute(stored_features, "wide", pair_swap(wide))
    t1, t2, t3 = pl.pallas_call(
        functools.partial(weights_kernel, wide),
        out_shape=(
            jax.ShapeDtypeStruct((4 * c1, 9 * 6 * c1), jnp.bfloat16),
            jax.ShapeDtypeStruct((2 * c2, 9 * 4 * c1), jnp.bfloat16),
            jax.ShapeDtypeStruct((9 * o3, 3 * c2), jnp.bfloat16),
        ),
        in_specs=[VMEM] * 3,
        out_specs=(VMEM,) * 3,
        compiler_params=params,
        cost_estimate=cost(10**6, 4 * 10**6),
    )(first_weight, second_weight, third_weight)
    own_slab = unpack(stored_features)
    pair_slab = unpack(pair)
    far, t1, t2, t3 = lax.optimization_barrier((far, t1, t2, t3))
    slab, relay, side = pl.pallas_call(
        functools.partial(slab_kernel, wide),
        out_shape=(
            jax.ShapeDtypeStruct((6 * c1, columns), jnp.bfloat16),
            jax.ShapeDtypeStruct((6 * c1, columns // 2), jnp.bfloat16),
            jax.ShapeDtypeStruct((6 * c1, columns // 2), jnp.bfloat16),
        ),
        in_specs=[VMEM] * 5,
        out_specs=(VMEM,) * 3,
        scratch_shapes=[pltpu.VMEM((rows, width), jnp.float32)],
        compiler_params=params,
        cost_estimate=cost(10**6, 2 * 10**6),
    )(far.reshape(rows, width), scale, shift, own_slab, pair_slab)
    crossed_rows = lax.ppermute(relay, BOTH, cross_narrow(wide, narrow))
    p1, hidden = pl.pallas_call(
        centre_kernel,
        out_shape=(
            jax.ShapeDtypeStruct((4 * c1, 4 * width), jnp.float32),
            jax.ShapeDtypeStruct((12 * c1, 2 * width), jnp.bfloat16),
        ),
        in_specs=[VMEM] * 2,
        out_specs=(VMEM,) * 2,
        scratch_shapes=[pltpu.VMEM((18 * c1, 4 * width), jnp.bfloat16)],
        compiler_params=params,
        cost_estimate=cost(10**7, 10**5),
    )(slab, t1)
    partner_rows = lax.ppermute(side, "narrow", pair_swap(narrow))
    p2 = pl.pallas_call(
        second_kernel,
        out_shape=jax.ShapeDtypeStruct((2 * c2, 4 * width), jnp.float32),
        in_specs=[VMEM] * 2,
        out_specs=VMEM,
        compiler_params=params,
        cost_estimate=cost(10**7, 10**5),
    )(hidden, t2)

    def add_side(kernel, out, rows, before):
        return pl.pallas_call(
            functools.partial(kernel, narrow),
            out_shape=out,
            in_specs=[VMEM] * 5,
            out_specs=VMEM,
            scratch_shapes=[
                pltpu.VMEM((18 * c1, 2 * width), jnp.bfloat16),
                pltpu.VMEM((12 * c1, 2 * width), jnp.bfloat16),
            ],
            compiler_params=params,
            cost_estimate=cost(10**7, 10**5),
        )(rows, p1, before, t1, t2)

    p2 = add_side(partner_kernel, jax.ShapeDtypeStruct(p2.shape, p2.dtype), partner_rows, p2)
    pooled = add_side(edge_kernel, jax.ShapeDtypeStruct((c2, LANES), jnp.bfloat16), crossed_rows, p2)
    pooled_far = lax.ppermute(pooled, BOTH, cross_wide(wide, narrow))
    pooled_pair = lax.ppermute(pooled, "wide", pair_swap(wide))
    mine = jnp.stack([pooled, pooled_pair, pooled_far])[None]
    held, held_places = mine, [0]
    arrivals = [(mine, [0]), (lax.ppermute(mine, "narrow", pair_swap(narrow)), [1])]
    bit = narrow // 2
    while bit > 1:
        other = lax.ppermute(held, "narrow", pair_swap(narrow, bit))
        places = [place ^ bit for place in held_places]
        arrivals.append((other, places))
        arrivals.append(
            (lax.ppermute(other, "narrow", pair_swap(narrow)), [place ^ 1 for place in places])
        )
        if bit > 2:
            held = jnp.concatenate([held, other])
        held_places = held_places + places
        bit //= 2
    total = narrow * LANES
    products = jax.ShapeDtypeStruct((9 * o3, total), jnp.float32)
    z = None
    for group in (arrivals[:2], arrivals[2:-1], arrivals[-1:]):
        if not group:
            continue
        places = [place for _, several in group for place in several]
        operands = [array for array, _ in group] + [t3] + ([] if z is None else [z])
        scratch = [pltpu.VMEM((3 * c2, len(places) * LANES), jnp.bfloat16)]
        common = dict(
            in_specs=[VMEM] * len(operands),
            scratch_shapes=scratch,
            compiler_params=params,
            cost_estimate=cost(10**7, 10**5),
        )
        if group[-1] is not arrivals[-1]:
            z = pl.pallas_call(
                functools.partial(
                    first_products_kernel if z is None else more_products_kernel, places
                ),
                out_shape=products,
                out_specs=VMEM,
                input_output_aliases={} if z is None else {len(operands) - 1: 0},
                **common,
            )(*operands)
        else:
            coarse, _ = pl.pallas_call(
                functools.partial(coarse_kernel, places),
                out_shape=(jax.ShapeDtypeStruct((o3, total), jnp.bfloat16), products),
                out_specs=(VMEM,) * 2,
                input_output_aliases={len(operands) - 1: 1},
                **common,
            )(*operands)
    return coarse[:, None, :]


def solution(mesh):
    in_specs = (P(None, "wide", "narrow", None), P(), P(), P(), P(), P("narrow", None))
    out_specs = P("narrow", "wide", None)
    return jax.shard_map(
        functools.partial(body, mesh.shape["wide"], mesh.shape["narrow"]),
        mesh=mesh,
        in_specs=in_specs,
        out_specs=out_specs,
        check_vma=False,
    )
```

```python
import functools

import jax
import jax.numpy as jnp
from jax import lax
from jax.experimental import pallas as pl
from jax.experimental.pallas import tpu as pltpu
from jax.sharding import PartitionSpec as P

LANES = 128
VMEM = pl.BlockSpec(memory_space=pltpu.VMEM)


def pair_swap(count, bit=1):
    return [(k, k ^ bit) for k in range(count)]


BOTH = ("wide", "narrow")


def crossing(position, count):
    target = position + 1 if position % 2 else position - 1
    return target if 0 <= target < count else None


def cross_wide(wide, narrow):
    bit = 2 if narrow % 4 == 0 else 1
    steps = []
    for i in range(wide):
        for j in range(narrow):
            target = crossing(i, wide)
            end = i * narrow + (j ^ bit) if target is None else target * narrow + j
            steps.append((i * narrow + j, end))
    return steps


def cross_narrow(wide, narrow, ends_meet):
    steps = []
    for i in range(wide):
        for j in range(narrow):
            target = crossing(j, narrow)
            if target is None:
                end = i * narrow + narrow - 1 - j if ends_meet else (i ^ 1) * narrow + j
            else:
                end = i * narrow + target
            steps.append((i * narrow + j, end))
    return steps


def weights_kernel(wide, w1_ref, w2_ref, w3_ref, t1_ref, t2_ref, t3_ref):
    i = lax.axis_index("wide")
    keep_low = jnp.where(i == 0, 0.0, 1.0)
    keep_high = jnp.where(i == wide - 1, 0.0, 1.0)

    def kept(value, keep):
        return (value.astype(jnp.float32) * keep).astype(jnp.bfloat16)

    o1 = w1_ref.shape[0]
    c1 = w1_ref.shape[1] // 27
    o2 = w2_ref.shape[0]
    c2 = w2_ref.shape[1] // 27
    o3 = w3_ref.shape[0]
    c3 = w3_ref.shape[1] // 27
    for ref, out, o, c, rows in ((w1_ref, t1_ref, o1, c1, 4), (w2_ref, t2_ref, o2, c2, 2)):
        span = (rows + 2) * c
        for be in range(9):
            taps = [ref[:, (a * 9 + be) * c : (a * 9 + be + 1) * c] for a in range(3)]
            for row in range(rows):
                parts = []
                if row:
                    parts.append(jnp.zeros((o, row * c), jnp.bfloat16))
                parts += taps
                if row < rows - 1:
                    parts.append(jnp.zeros((o, (rows - 1 - row) * c), jnp.bfloat16))
                value = jnp.concatenate(parts, axis=1)
                if rows == 4 and row in (0, 3):
                    value = kept(value, keep_low if row == 0 else keep_high)
                out[row * o : (row + 1) * o, be * span : (be + 1) * span] = value
    for be in range(9):
        for a in range(3):
            value = w3_ref[:, (a * 9 + be) * c3 : (a * 9 + be + 1) * c3]
            if a != 1:
                value = kept(value, keep_low if a == 0 else keep_high)
            t3_ref[be * o3 : (be + 1) * o3, a * c3 : (a + 1) * c3] = value


def shifted(value):
    lane = lax.broadcasted_iota(jnp.int32, value.shape, 1)
    low = jnp.where(lane == 0, 0.0, pltpu.roll(value, 1, 1))
    high = jnp.where(lane == LANES - 1, 0.0, pltpu.roll(value, LANES - 1, 1))
    return low, value, high


def column(row_ref):
    row = row_ref[...]
    square = (row.shape[1], row.shape[1])
    here = lax.broadcasted_iota(jnp.int32, square, 0) == lax.broadcasted_iota(jnp.int32, square, 1)
    return jnp.sum(jnp.where(here, jnp.broadcast_to(row, square), 0.0), axis=1, keepdims=True)


def unpack_kernel(raw_ref, scale_ref, shift_ref, out_ref, staged):
    c = scale_ref.shape[1]
    depth, height = out_ref.shape[0] // c, out_ref.shape[1] // LANES
    staged[...] = raw_ref[...].astype(jnp.float32)
    scale, shift = column(scale_ref), column(shift_ref)
    for d in range(depth):
        for h in range(height):
            rows = staged[pl.ds(d * height + h, c, stride=depth * height), :]
            out_ref[d * c : (d + 1) * c, h * LANES : (h + 1) * LANES] = (
                rows * scale + shift
            ).astype(jnp.bfloat16)


def slab_kernel(
    wide, raw_ref, scale_ref, shift_ref, own_ref, pair_ref, out_ref, relay_ref, side_ref, staged
):
    i, j = lax.axis_index("wide"), lax.axis_index("narrow")
    i_odd, j_odd = lax.rem(i, 2), lax.rem(j, 2)
    block, columns = own_ref.shape
    c = scale_ref.shape[1]
    depth, height = block // c, columns // LANES
    far_row = pl.multiple_of(2 * i_odd * block, block)
    pair_row = pl.multiple_of((2 - 2 * i_odd) * block, block)
    keep = jnp.where(i == i_odd * (wide - 1), 0.0, 1.0)
    staged[...] = raw_ref[...].astype(jnp.float32)
    scale, shift = column(scale_ref) * keep, column(shift_ref) * keep
    for d in range(depth):
        for h in range(height):
            rows = staged[pl.ds(d * height + h, c, stride=depth * height), :]
            out_ref[
                pl.ds(pl.multiple_of(far_row + d * c, c), c), h * LANES : (h + 1) * LANES
            ] = (rows * scale + shift).astype(jnp.bfloat16)
    out_ref[block : 2 * block, :] = own_ref[...]
    out_ref[pl.ds(pair_row, block), :] = pair_ref[...]
    half = columns // 2
    lane = pl.multiple_of(j_odd * half, half)
    relay_ref[:block, :] = out_ref[:block, pl.ds(lane, half)]
    relay_ref[block:, :] = out_ref[2 * block :, pl.ds(lane, half)]
    side_ref[...] = out_ref[:, pl.ds(pl.multiple_of((1 - j_odd) * half, half), half)]


def dot(a, b):
    return jnp.dot(a, b, preferred_element_type=jnp.float32)


def tile(ref, *picks):
    return jnp.concatenate([ref[:, k * LANES : (k + 1) * LANES] for k in picks], axis=1)


def spread(value, ref, at):
    rows, columns = value.shape
    for k in range(columns // LANES):
        parts = shifted(value[:, k * LANES : (k + 1) * LANES].astype(jnp.float32))
        for e, part in enumerate(parts):
            ref[e * rows : (e + 1) * rows, pl.ds(at + k * LANES, LANES)] = part.astype(jnp.bfloat16)


def thirds(ref):
    span = ref.shape[1] // 3
    return [ref[:, b * span : (b + 1) * span] for b in range(3)]


def centre_kernel(x_ref, w1_ref, p1_ref, hidden_ref, taps):
    spread(x_ref[...], taps, 0)
    first = thirds(w1_ref)
    columns = jnp.concatenate(
        [taps[:, b * LANES : (b + 2) * LANES] for b in range(3)], axis=0
    )
    spread(jnp.maximum(dot(w1_ref[...], columns), 0.0), hidden_ref, 0)
    r0 = dot(first[0], tile(taps, 2, 3))
    r1 = dot(first[1], tile(taps, 0, 3))
    r2 = dot(first[2], tile(taps, 0, 1))
    p1_ref[:, 0:LANES] = r2[:, :LANES]
    p1_ref[:, LANES : 2 * LANES] = r2[:, LANES:] + r1[:, :LANES]
    p1_ref[:, 2 * LANES : 3 * LANES] = r0[:, LANES:]
    p1_ref[:, 3 * LANES :] = r1[:, LANES:] + r0[:, :LANES]


def second_kernel(hidden_ref, w2_ref, p2_ref):
    both = hidden_ref[...]
    q0, q1, q2 = (dot(w, both) for w in thirds(w2_ref))
    p2_ref[:, 0:LANES] = q2[:, :LANES]
    p2_ref[:, LANES : 2 * LANES] = q2[:, LANES:] + q1[:, :LANES]
    p2_ref[:, 2 * LANES : 3 * LANES] = q0[:, LANES:]
    p2_ref[:, 3 * LANES :] = q1[:, LANES:] + q0[:, :LANES]


def stacked(value):
    return jnp.concatenate([part.astype(jnp.bfloat16) for part in shifted(value)], axis=0)


def side_terms(high, keep, feature, p1_ref, w1_ref, w2_ref):
    span1, span2 = w1_ref.shape[1] // 3, w2_ref.shape[1] // 3
    outer1, outer2 = pl.multiple_of(2 * high * span1, LANES), pl.multiple_of(2 * high * span2, LANES)
    taps = jnp.concatenate([stacked(feature(k)) for k in range(2)], axis=1)
    r = dot(w1_ref[:, pl.ds(outer1, span1)], taps)
    r1 = dot(w1_ref[:, span1 : 2 * span1], taps)
    up = high == 1
    before = p1_ref[:, pl.ds(pl.multiple_of(high * 2 * LANES, LANES), 2 * LANES)]
    end = jnp.where(up, r[:, LANES:] + r1[:, :LANES], r[:, :LANES] + r1[:, LANES:])
    end = jnp.maximum(end + before[:, :LANES], 0.0)
    end = stacked(end if keep is None else end * keep)
    near = jnp.where(up, r[:, :LANES], r[:, LANES:])
    near = stacked(jnp.maximum(near + before[:, LANES:], 0.0))
    q = dot(w2_ref[:, pl.ds(outer2, span2)], jnp.concatenate([end, near], axis=1))
    q1 = dot(w2_ref[:, span2 : 2 * span2], near)
    return q[:, :LANES] + q1, q[:, LANES:]


def partner_kernel(rows_ref, p1_ref, p2_ref, w1_ref, w2_ref, out_ref):
    high = 1 - lax.rem(lax.axis_index("narrow"), 2)

    def feature(k):
        return rows_ref[:, k * LANES : (k + 1) * LANES].astype(jnp.float32)

    end, near = side_terms(high, None, feature, p1_ref, w1_ref, w2_ref)
    at = pl.multiple_of(high * 2 * LANES, LANES)
    out_ref[...] = p2_ref[...]
    out_ref[:, pl.ds(at, LANES)] += end
    out_ref[:, pl.ds(at + LANES, LANES)] += near


def edge_kernel(
    narrow, own_ref, rows_ref, scale_ref, shift_ref, p1_ref, p2_ref, w1_ref, w2_ref, out_ref, staged
):
    j = lax.axis_index("narrow")
    high = lax.rem(j, 2)
    keep = jnp.where(j == high * (narrow - 1), 0.0, 1.0)
    staged[...] = own_ref[...].astype(jnp.float32)
    scale, shift = column(scale_ref) * keep, column(shift_ref) * keep
    c = scale.shape[0]

    def feature(k):
        rows = rows_ref[:, k * LANES : (k + 1) * LANES].astype(jnp.float32) * keep
        own = [staged[pl.ds(2 * d + k, c, stride=4), :] * scale + shift for d in range(2)]
        return jnp.concatenate([rows[: 2 * c]] + own + [rows[2 * c :]], axis=0)

    end, near = side_terms(high, keep, feature, p1_ref, w1_ref, w2_ref)
    c2 = out_ref.shape[0]
    at = pl.multiple_of(high * 2 * LANES, LANES)
    other = pl.multiple_of((1 - high) * 2 * LANES, LANES)

    def best(one, two):
        value = jnp.maximum(one, two)
        value = jnp.maximum(jnp.maximum(value[:c2], value[c2:]), 0.0)
        return jnp.maximum(value, pltpu.roll(value, LANES - 1, 1)).astype(jnp.bfloat16)

    mine = best(end + p2_ref[:, pl.ds(at, LANES)], near + p2_ref[:, pl.ds(at + LANES, LANES)])
    rest = best(p2_ref[:, pl.ds(other, LANES)], p2_ref[:, pl.ds(other + LANES, LANES)])
    cell = lax.broadcasted_iota(jnp.int32, (2 * LANES, LANES), 0)
    target = lax.broadcasted_iota(jnp.int32, (2 * LANES, LANES), 1)
    wanted = jnp.bitwise_xor(2 * target, high * LANES)
    pick = (cell == wanted).astype(jnp.bfloat16)
    out_ref[...] = dot(jnp.concatenate([mine, rest], axis=1), pick).astype(jnp.bfloat16)


def coarse_products(places, blocks, w3_ref, z_ref, slab):
    i, j = lax.axis_index("wide"), lax.axis_index("narrow")
    i_odd = lax.rem(i, 2)
    slots = (1, 2 - 2 * i_odd, 2 * i_odd)
    at = 0
    for ref in blocks:
        for r in range(ref.shape[0]):
            for k in range(3):
                row = pl.multiple_of(slots[k] * ref.shape[2], ref.shape[2])
                slab[pl.ds(row, ref.shape[2]), at : at + LANES] = ref[r, k]
            at += LANES
    z = dot(w3_ref[...], slab[...])
    for k, place in enumerate(places):
        lane = pl.multiple_of(jnp.bitwise_xor(j, place) * LANES, LANES)
        z_ref[:, pl.ds(lane, LANES)] = z[:, k * LANES : (k + 1) * LANES]


def first_products_kernel(places, *refs):
    *blocks, w3_ref, z_ref, slab = refs
    coarse_products(places, blocks, w3_ref, z_ref, slab)


def more_products_kernel(places, *refs):
    *blocks, w3_ref, _, z_ref, slab = refs
    coarse_products(places, blocks, w3_ref, z_ref, slab)


def coarse_kernel(places, blocks_ref, w3_ref, before_ref, out_ref, z_ref, slab):
    del before_ref
    coarse_products(places, [blocks_ref], w3_ref, z_ref, slab)
    o, total = out_ref.shape
    width = LANES // 2
    count = total // LANES
    lane = lax.broadcasted_iota(jnp.int32, (o, LANES), 1)
    column_of = lax.rem(lane, width)

    def z(b, e, q):
        if q < 0 or q >= count:
            return jnp.zeros((o, LANES), jnp.float32)
        at = (b * 3 + e) * o
        return z_ref[at : at + o, q * LANES : (q + 1) * LANES]

    for q in range(count):
        terms = []
        for e in range(3):
            crossed = jnp.where(
                lane < width, z(0, e, q) + z(2, e, q + 1), z(0, e, q - 1) + z(2, e, q)
            )
            terms.append(z(1, e, q) + pltpu.roll(crossed, width, 1))
        low = jnp.where(column_of == 0, 0.0, pltpu.roll(terms[0], 1, 1))
        high = jnp.where(column_of == width - 1, 0.0, pltpu.roll(terms[2], LANES - 1, 1))
        out_ref[:, q * LANES : (q + 1) * LANES] = jnp.maximum(low + terms[1] + high, 0.0).astype(
            jnp.bfloat16
        )


def body(
    wide, narrow, stored_features, channel_scale, channel_shift, first_weight, second_weight,
    third_weight,
):
    c1, depth, height, width = stored_features.shape
    c2 = second_weight.shape[0]
    o3 = third_weight.shape[0]
    params = pltpu.CompilerParams(vmem_limit_bytes=24 * 1024 * 1024)
    rows = c1 * depth * height
    columns = height * width
    scale, shift = channel_scale.reshape(1, c1), channel_shift.reshape(1, c1)

    def cost(flops, size):
        return pl.CostEstimate(flops=flops, bytes_accessed=size, transcendentals=0)

    def unpack(block):
        return pl.pallas_call(
            unpack_kernel,
            out_shape=jax.ShapeDtypeStruct((depth * c1, columns), jnp.bfloat16),
            in_specs=[VMEM] * 3,
            out_specs=VMEM,
            scratch_shapes=[pltpu.VMEM((rows, width), jnp.float32)],
            compiler_params=params,
            cost_estimate=cost(10**6, 10**6),
        )(block.reshape(rows, width), scale, shift)

    far = lax.ppermute(stored_features, BOTH, cross_wide(wide, narrow))
    pair = lax.ppermute(stored_features, "wide", pair_swap(wide))
    t1, t2, t3 = pl.pallas_call(
        functools.partial(weights_kernel, wide),
        out_shape=(
            jax.ShapeDtypeStruct((4 * c1, 9 * 6 * c1), jnp.bfloat16),
            jax.ShapeDtypeStruct((2 * c2, 9 * 4 * c1), jnp.bfloat16),
            jax.ShapeDtypeStruct((9 * o3, 3 * c2), jnp.bfloat16),
        ),
        in_specs=[VMEM] * 3,
        out_specs=(VMEM,) * 3,
        compiler_params=params,
        cost_estimate=cost(10**6, 4 * 10**6),
    )(first_weight, second_weight, third_weight)
    half = height // 2
    edges = jnp.where(
        lax.axis_index("narrow") % 2 == 1,
        stored_features[:, :, half:],
        stored_features[:, :, :half],
    )
    crossed_own = lax.ppermute(edges, BOTH, cross_narrow(wide, narrow, True))
    pair, raw, scale, shift = lax.optimization_barrier((pair, stored_features, scale, shift))
    own_slab = unpack(raw)
    pair_slab = unpack(pair)
    far, pair_slab, t1, t2, t3 = lax.optimization_barrier((far, pair_slab, t1, t2, t3))
    slab, relay, side = pl.pallas_call(
        functools.partial(slab_kernel, wide),
        out_shape=(
            jax.ShapeDtypeStruct((6 * c1, columns), jnp.bfloat16),
            jax.ShapeDtypeStruct((4 * c1, columns // 2), jnp.bfloat16),
            jax.ShapeDtypeStruct((6 * c1, columns // 2), jnp.bfloat16),
        ),
        in_specs=[VMEM] * 5,
        out_specs=(VMEM,) * 3,
        scratch_shapes=[pltpu.VMEM((rows, width), jnp.float32)],
        compiler_params=params,
        cost_estimate=cost(10**6, 2 * 10**6),
    )(far.reshape(rows, width), scale, shift, own_slab, pair_slab)
    relay, side, crossed_own = lax.optimization_barrier((relay, side, crossed_own))
    crossed_rows = lax.ppermute(relay, BOTH, cross_narrow(wide, narrow, False))
    p1, hidden = pl.pallas_call(
        centre_kernel,
        out_shape=(
            jax.ShapeDtypeStruct((4 * c1, 4 * width), jnp.float32),
            jax.ShapeDtypeStruct((12 * c1, 2 * width), jnp.bfloat16),
        ),
        in_specs=[VMEM] * 2,
        out_specs=(VMEM,) * 2,
        scratch_shapes=[pltpu.VMEM((18 * c1, 4 * width), jnp.bfloat16)],
        compiler_params=params,
        cost_estimate=cost(10**7, 10**5),
    )(slab, t1)
    partner_rows = lax.ppermute(side, "narrow", pair_swap(narrow))
    p2 = pl.pallas_call(
        second_kernel,
        out_shape=jax.ShapeDtypeStruct((2 * c2, 4 * width), jnp.float32),
        in_specs=[VMEM] * 2,
        out_specs=VMEM,
        compiler_params=params,
        cost_estimate=cost(10**7, 10**5),
    )(hidden, t2)

    p2 = pl.pallas_call(
        partner_kernel,
        out_shape=jax.ShapeDtypeStruct(p2.shape, p2.dtype),
        in_specs=[VMEM] * 5,
        out_specs=VMEM,
        compiler_params=params,
        cost_estimate=cost(10**7, 10**5),
    )(partner_rows, p1, p2, t1, t2)
    pooled = pl.pallas_call(
        functools.partial(edge_kernel, narrow),
        out_shape=jax.ShapeDtypeStruct((c2, LANES), jnp.bfloat16),
        in_specs=[VMEM] * 8,
        out_specs=VMEM,
        scratch_shapes=[pltpu.VMEM((rows // 2, width), jnp.float32)],
        compiler_params=params,
        cost_estimate=cost(10**7, 10**5),
    )(crossed_own.reshape(rows // 2, width), crossed_rows, scale, shift, p1, p2, t1, t2)
    pooled_far = lax.ppermute(pooled, BOTH, cross_wide(wide, narrow))
    pooled_pair = lax.ppermute(pooled, "wide", pair_swap(wide))
    mine = jnp.stack([pooled, pooled_pair, pooled_far])[None]
    held, held_places = mine, [0]
    arrivals = [(mine, [0]), (lax.ppermute(mine, "narrow", pair_swap(narrow)), [1])]
    bit = narrow // 2
    while bit > 1:
        other = lax.ppermute(held, "narrow", pair_swap(narrow, bit))
        places = [place ^ bit for place in held_places]
        arrivals.append((other, places))
        arrivals.append(
            (lax.ppermute(other, "narrow", pair_swap(narrow)), [place ^ 1 for place in places])
        )
        if bit > 2:
            held = jnp.concatenate([held, other])
        held_places = held_places + places
        bit //= 2
    total = narrow * LANES
    products = jax.ShapeDtypeStruct((9 * o3, total), jnp.float32)
    z = None
    for group in (arrivals[:2], arrivals[2:-1], arrivals[-1:]):
        if not group:
            continue
        places = [place for _, several in group for place in several]
        operands = [array for array, _ in group] + [t3] + ([] if z is None else [z])
        scratch = [pltpu.VMEM((3 * c2, len(places) * LANES), jnp.bfloat16)]
        common = dict(
            in_specs=[VMEM] * len(operands),
            scratch_shapes=scratch,
            compiler_params=params,
            cost_estimate=cost(10**7, 10**5),
        )
        if group[-1] is not arrivals[-1]:
            z = pl.pallas_call(
                functools.partial(
                    first_products_kernel if z is None else more_products_kernel, places
                ),
                out_shape=products,
                out_specs=VMEM,
                input_output_aliases={} if z is None else {len(operands) - 1: 0},
                **common,
            )(*operands)
        else:
            coarse, _ = pl.pallas_call(
                functools.partial(coarse_kernel, places),
                out_shape=(jax.ShapeDtypeStruct((o3, total), jnp.bfloat16), products),
                out_specs=(VMEM,) * 2,
                input_output_aliases={len(operands) - 1: 1},
                **common,
            )(*operands)
    return coarse[:, None, :]


def solution(mesh):
    in_specs = (P(None, "wide", "narrow", None), P(), P(), P(), P(), P("narrow", None))
    out_specs = P("narrow", "wide", None)
    return jax.shard_map(
        functools.partial(body, mesh.shape["wide"], mesh.shape["narrow"]),
        mesh=mesh,
        in_specs=in_specs,
        out_specs=out_specs,
        check_vma=False,
    )
```

```python
import functools

import jax
import jax.numpy as jnp
from jax import lax
from jax.experimental import pallas as pl
from jax.experimental.pallas import tpu as pltpu
from jax.sharding import PartitionSpec as P

LANES = 128
VMEM = pl.BlockSpec(memory_space=pltpu.VMEM)


def pair_swap(count, bit=1):
    return [(k, k ^ bit) for k in range(count)]


BOTH = ("wide", "narrow")


def crossing(position, count):
    target = position + 1 if position % 2 else position - 1
    return target if 0 <= target < count else None


def cross_wide(wide, narrow):
    bit = 1
    steps = []
    for i in range(wide):
        for j in range(narrow):
            target = crossing(i, wide)
            end = i * narrow + (j ^ bit) if target is None else target * narrow + j
            steps.append((i * narrow + j, end))
    return steps


def cross_narrow(wide, narrow, ends_meet):
    steps = []
    for i in range(wide):
        for j in range(narrow):
            target = crossing(j, narrow)
            if target is None:
                end = i * narrow + narrow - 1 - j if ends_meet else (i ^ 1) * narrow + j
            else:
                end = i * narrow + target
            steps.append((i * narrow + j, end))
    return steps


def weights_kernel(wide, w1_ref, w2_ref, w3_ref, t1_ref, t2_ref, t3_ref):
    i = lax.axis_index("wide")
    keep_low = jnp.where(i == 0, 0.0, 1.0)
    keep_high = jnp.where(i == wide - 1, 0.0, 1.0)

    def kept(value, keep):
        return (value.astype(jnp.float32) * keep).astype(jnp.bfloat16)

    o1 = w1_ref.shape[0]
    c1 = w1_ref.shape[1] // 27
    o2 = w2_ref.shape[0]
    c2 = w2_ref.shape[1] // 27
    o3 = w3_ref.shape[0]
    c3 = w3_ref.shape[1] // 27
    for ref, out, o, c, rows in ((w1_ref, t1_ref, o1, c1, 4), (w2_ref, t2_ref, o2, c2, 2)):
        span = (rows + 2) * c
        for be in range(9):
            taps = [ref[:, (a * 9 + be) * c : (a * 9 + be + 1) * c] for a in range(3)]
            for row in range(rows):
                parts = []
                if row:
                    parts.append(jnp.zeros((o, row * c), jnp.bfloat16))
                parts += taps
                if row < rows - 1:
                    parts.append(jnp.zeros((o, (rows - 1 - row) * c), jnp.bfloat16))
                value = jnp.concatenate(parts, axis=1)
                if rows == 4 and row in (0, 3):
                    value = kept(value, keep_low if row == 0 else keep_high)
                out[row * o : (row + 1) * o, be * span : (be + 1) * span] = value
    for be in range(9):
        for a in range(3):
            value = w3_ref[:, (a * 9 + be) * c3 : (a * 9 + be + 1) * c3]
            if a != 1:
                value = kept(value, keep_low if a == 0 else keep_high)
            t3_ref[be * o3 : (be + 1) * o3, a * c3 : (a + 1) * c3] = value


def shifted(value):
    lane = lax.broadcasted_iota(jnp.int32, value.shape, 1)
    low = jnp.where(lane == 0, 0.0, pltpu.roll(value, 1, 1))
    high = jnp.where(lane == LANES - 1, 0.0, pltpu.roll(value, LANES - 1, 1))
    return low, value, high


def column(row_ref):
    row = row_ref[...]
    square = (row.shape[1], row.shape[1])
    here = lax.broadcasted_iota(jnp.int32, square, 0) == lax.broadcasted_iota(jnp.int32, square, 1)
    return jnp.sum(jnp.where(here, jnp.broadcast_to(row, square), 0.0), axis=1, keepdims=True)


def slab_kernel(
    wide, own_ref, pair_ref, far_ref, scale_ref, shift_ref, out_ref, relay_ref, side_ref, staged
):
    i, j = lax.axis_index("wide"), lax.axis_index("narrow")
    i_odd, j_odd = lax.rem(i, 2), lax.rem(j, 2)
    block, columns = out_ref.shape[0] // 3, out_ref.shape[1]
    c = scale_ref.shape[1]
    depth, height = block // c, columns // LANES
    keep = jnp.where(i == i_odd * (wide - 1), 0.0, 1.0)
    scale, shift = column(scale_ref), column(shift_ref)
    size = own_ref.shape[0]
    for n, ref in enumerate((own_ref, pair_ref, far_ref)):
        staged[n * size : (n + 1) * size, :] = ref[...].astype(jnp.float32)
        slot = (1, 2 - 2 * i_odd, 2 * i_odd)[n]
        gain, offset = (scale * keep, shift * keep) if n == 2 else (scale, shift)
        for d in range(depth):
            for h in range(height):
                start = n * size + d * height + h
                value = staged[pl.ds(start, c, stride=depth * height), :] * gain + offset
                row = slot * block + d * c
                rows = slice(row, row + c) if n == 0 else pl.ds(pl.multiple_of(row, c), c)
                out_ref[rows, h * LANES : (h + 1) * LANES] = value.astype(jnp.bfloat16)

    half = columns // 2
    lane = pl.multiple_of(j_odd * half, half)
    relay_ref[:block, :] = out_ref[:block, pl.ds(lane, half)]
    relay_ref[block:, :] = out_ref[2 * block :, pl.ds(lane, half)]
    side_ref[...] = out_ref[:, pl.ds(pl.multiple_of((1 - j_odd) * half, half), half)]


def dot(a, b):
    return jnp.dot(a, b, preferred_element_type=jnp.float32)


def tile(ref, *picks):
    return jnp.concatenate([ref[:, k * LANES : (k + 1) * LANES] for k in picks], axis=1)


def spread(value, ref, at):
    rows, columns = value.shape
    for k in range(columns // LANES):
        parts = shifted(value[:, k * LANES : (k + 1) * LANES].astype(jnp.float32))
        for e, part in enumerate(parts):
            ref[e * rows : (e + 1) * rows, pl.ds(at + k * LANES, LANES)] = part.astype(jnp.bfloat16)


def thirds(ref):
    span = ref.shape[1] // 3
    return [ref[:, b * span : (b + 1) * span] for b in range(3)]


def beside(*parts):
    return jnp.concatenate(parts, axis=1)


def part(ref, k):
    return ref[:, k * LANES : (k + 1) * LANES]


def centre_kernel(x_ref, w1_ref, w2_ref, p1_ref, p2_ref):
    taps = [stacked(part(x_ref, k).astype(jnp.float32)) for k in range(4)]
    first = thirds(w1_ref)
    pairs = jnp.concatenate([beside(taps[b], taps[b + 1]) for b in range(3)], axis=0)
    inner = jnp.maximum(dot(w1_ref[...], pairs), 0.0)
    both = beside(stacked(inner[:, :LANES]), stacked(inner[:, LANES:]))
    r0 = dot(first[0], beside(taps[2], taps[3]))
    r1 = dot(first[1], beside(taps[0], taps[3]))
    r2 = dot(first[2], beside(taps[0], taps[1]))
    p1_ref[:, 0:LANES] = r2[:, :LANES]
    p1_ref[:, LANES : 2 * LANES] = r2[:, LANES:] + r1[:, :LANES]
    p1_ref[:, 2 * LANES : 3 * LANES] = r0[:, LANES:]
    p1_ref[:, 3 * LANES :] = r1[:, LANES:] + r0[:, :LANES]
    q0, q1, q2 = (dot(w, both) for w in thirds(w2_ref))
    p2_ref[:, 0:LANES] = q2[:, :LANES]
    p2_ref[:, LANES : 2 * LANES] = q2[:, LANES:] + q1[:, :LANES]
    p2_ref[:, 2 * LANES : 3 * LANES] = q0[:, LANES:]
    p2_ref[:, 3 * LANES :] = q1[:, LANES:] + q0[:, :LANES]


def stacked(value):
    return jnp.concatenate([part.astype(jnp.bfloat16) for part in shifted(value)], axis=0)


def side_terms(high, keep, feature, p1_ref, w1_ref, w2_ref):
    span1, span2 = w1_ref.shape[1] // 3, w2_ref.shape[1] // 3
    outer1, outer2 = pl.multiple_of(2 * high * span1, LANES), pl.multiple_of(2 * high * span2, LANES)
    taps = jnp.concatenate([stacked(feature(k)) for k in range(2)], axis=1)
    r = dot(w1_ref[:, pl.ds(outer1, span1)], taps)
    r1 = dot(w1_ref[:, span1 : 2 * span1], taps)
    up = high == 1
    before = p1_ref[:, pl.ds(pl.multiple_of(high * 2 * LANES, LANES), 2 * LANES)]
    end = jnp.where(up, r[:, LANES:] + r1[:, :LANES], r[:, :LANES] + r1[:, LANES:])
    end = jnp.maximum(end + before[:, :LANES], 0.0)
    end = stacked(end if keep is None else end * keep)
    near = jnp.where(up, r[:, :LANES], r[:, LANES:])
    near = stacked(jnp.maximum(near + before[:, LANES:], 0.0))
    q = dot(w2_ref[:, pl.ds(outer2, span2)], jnp.concatenate([end, near], axis=1))
    q1 = dot(w2_ref[:, span2 : 2 * span2], near)
    return q[:, :LANES] + q1, q[:, LANES:]


def partner_kernel(rows_ref, p1_ref, p2_ref, w1_ref, w2_ref, out_ref):
    high = 1 - lax.rem(lax.axis_index("narrow"), 2)

    def feature(k):
        return rows_ref[:, k * LANES : (k + 1) * LANES].astype(jnp.float32)

    end, near = side_terms(high, None, feature, p1_ref, w1_ref, w2_ref)
    at = pl.multiple_of(high * 2 * LANES, LANES)
    out_ref[...] = p2_ref[...]
    out_ref[:, pl.ds(at, LANES)] += end
    out_ref[:, pl.ds(at + LANES, LANES)] += near


def edge_kernel(
    narrow, own_ref, rows_ref, scale_ref, shift_ref, p1_ref, p2_ref, w1_ref, w2_ref, out_ref, staged
):
    j = lax.axis_index("narrow")
    high = lax.rem(j, 2)
    keep = jnp.where(j == high * (narrow - 1), 0.0, 1.0)
    staged[...] = own_ref[...].astype(jnp.float32)
    scale, shift = column(scale_ref) * keep, column(shift_ref) * keep
    c = scale.shape[0]

    def feature(k):
        rows = rows_ref[:, k * LANES : (k + 1) * LANES].astype(jnp.float32) * keep
        own = [staged[pl.ds(2 * d + k, c, stride=4), :] * scale + shift for d in range(2)]
        return jnp.concatenate([rows[: 2 * c]] + own + [rows[2 * c :]], axis=0)

    end, near = side_terms(high, keep, feature, p1_ref, w1_ref, w2_ref)
    c2 = out_ref.shape[0]
    at = pl.multiple_of(high * 2 * LANES, LANES)
    other = pl.multiple_of((1 - high) * 2 * LANES, LANES)

    def best(one, two):
        value = jnp.maximum(one, two)
        value = jnp.maximum(jnp.maximum(value[:c2], value[c2:]), 0.0)
        return jnp.maximum(value, pltpu.roll(value, LANES - 1, 1)).astype(jnp.bfloat16)

    mine = best(end + p2_ref[:, pl.ds(at, LANES)], near + p2_ref[:, pl.ds(at + LANES, LANES)])
    rest = best(p2_ref[:, pl.ds(other, LANES)], p2_ref[:, pl.ds(other + LANES, LANES)])
    cell = lax.broadcasted_iota(jnp.int32, (2 * LANES, LANES), 0)
    target = lax.broadcasted_iota(jnp.int32, (2 * LANES, LANES), 1)
    wanted = jnp.bitwise_xor(2 * target, high * LANES)
    pick = (cell == wanted).astype(jnp.bfloat16)
    out_ref[...] = dot(jnp.concatenate([mine, rest], axis=1), pick).astype(jnp.bfloat16)


def coarse_products(places, blocks, w3_ref, z_ref, slab):
    i, j = lax.axis_index("wide"), lax.axis_index("narrow")
    i_odd = lax.rem(i, 2)
    slots = (1, 2 - 2 * i_odd, 2 * i_odd)
    at = 0
    for ref in blocks:
        for r in range(ref.shape[0]):
            for k in range(3):
                row = pl.multiple_of(slots[k] * ref.shape[2], ref.shape[2])
                slab[pl.ds(row, ref.shape[2]), at : at + LANES] = ref[r, k]
            at += LANES
    z = dot(w3_ref[...], slab[...])
    for k, place in enumerate(places):
        lane = pl.multiple_of(jnp.bitwise_xor(j, place) * LANES, LANES)
        z_ref[:, pl.ds(lane, LANES)] = z[:, k * LANES : (k + 1) * LANES]


def first_products_kernel(places, *refs):
    *blocks, w3_ref, z_ref, slab = refs
    coarse_products(places, blocks, w3_ref, z_ref, slab)


def more_products_kernel(places, *refs):
    *blocks, w3_ref, _, z_ref, slab = refs
    coarse_products(places, blocks, w3_ref, z_ref, slab)


def coarse_kernel(places, blocks_ref, w3_ref, before_ref, out_ref, z_ref, slab):
    del before_ref
    coarse_products(places, [blocks_ref], w3_ref, z_ref, slab)
    o, total = out_ref.shape
    width = LANES // 2
    count = total // LANES
    lane = lax.broadcasted_iota(jnp.int32, (o, LANES), 1)
    column_of = lax.rem(lane, width)

    def z(b, e, q):
        if q < 0 or q >= count:
            return jnp.zeros((o, LANES), jnp.float32)
        at = (b * 3 + e) * o
        return z_ref[at : at + o, q * LANES : (q + 1) * LANES]

    for q in range(count):
        terms = []
        for e in range(3):
            crossed = jnp.where(
                lane < width, z(0, e, q) + z(2, e, q + 1), z(0, e, q - 1) + z(2, e, q)
            )
            terms.append(z(1, e, q) + pltpu.roll(crossed, width, 1))
        low = jnp.where(column_of == 0, 0.0, pltpu.roll(terms[0], 1, 1))
        high = jnp.where(column_of == width - 1, 0.0, pltpu.roll(terms[2], LANES - 1, 1))
        out_ref[:, q * LANES : (q + 1) * LANES] = jnp.maximum(low + terms[1] + high, 0.0).astype(
            jnp.bfloat16
        )


def body(
    wide, narrow, stored_features, channel_scale, channel_shift, first_weight, second_weight,
    third_weight,
):
    c1, depth, height, width = stored_features.shape
    c2 = second_weight.shape[0]
    o3 = third_weight.shape[0]
    params = pltpu.CompilerParams(vmem_limit_bytes=24 * 1024 * 1024)
    rows = c1 * depth * height
    columns = height * width
    scale, shift = channel_scale.reshape(1, c1), channel_shift.reshape(1, c1)

    def cost(flops, size):
        return pl.CostEstimate(flops=flops, bytes_accessed=size, transcendentals=0)

    far = lax.ppermute(stored_features, BOTH, cross_wide(wide, narrow))
    pair = lax.ppermute(stored_features, "wide", pair_swap(wide))
    t1, t2, t3 = pl.pallas_call(
        functools.partial(weights_kernel, wide),
        out_shape=(
            jax.ShapeDtypeStruct((4 * c1, 9 * 6 * c1), jnp.bfloat16),
            jax.ShapeDtypeStruct((2 * c2, 9 * 4 * c1), jnp.bfloat16),
            jax.ShapeDtypeStruct((9 * o3, 3 * c2), jnp.bfloat16),
        ),
        in_specs=[VMEM] * 3,
        out_specs=(VMEM,) * 3,
        compiler_params=params,
        cost_estimate=cost(10**6, 4 * 10**6),
    )(first_weight, second_weight, third_weight)
    half = height // 2
    edges = jnp.where(
        lax.axis_index("narrow") % 2 == 1,
        stored_features[:, :, half:],
        stored_features[:, :, :half],
    )
    crossed_own = lax.ppermute(edges, BOTH, cross_narrow(wide, narrow, True))
    pair, raw, scale, shift = lax.optimization_barrier((pair, stored_features, scale, shift))
    pair_rows = pair.reshape(rows, width)
    far, pair_rows, t1, t2, t3 = lax.optimization_barrier((far, pair_rows, t1, t2, t3))
    slab, relay, side = pl.pallas_call(
        functools.partial(slab_kernel, wide),
        out_shape=(
            jax.ShapeDtypeStruct((6 * c1, columns), jnp.bfloat16),
            jax.ShapeDtypeStruct((4 * c1, columns // 2), jnp.bfloat16),
            jax.ShapeDtypeStruct((6 * c1, columns // 2), jnp.bfloat16),
        ),
        in_specs=[VMEM] * 5,
        out_specs=(VMEM,) * 3,
        scratch_shapes=[pltpu.VMEM((3 * rows, width), jnp.float32)],
        compiler_params=params,
        cost_estimate=cost(10**6, 2 * 10**6),
    )(raw.reshape(rows, width), pair_rows, far.reshape(rows, width), scale, shift)
    relay, side, crossed_own = lax.optimization_barrier((relay, side, crossed_own))
    crossed_rows = lax.ppermute(relay, BOTH, cross_narrow(wide, narrow, False))
    p1, p2 = pl.pallas_call(
        centre_kernel,
        out_shape=(
            jax.ShapeDtypeStruct((4 * c1, 4 * width), jnp.float32),
            jax.ShapeDtypeStruct((2 * c2, 4 * width), jnp.float32),
        ),
        in_specs=[VMEM] * 3,
        out_specs=(VMEM,) * 2,
        compiler_params=params,
        cost_estimate=cost(10**7, 10**5),
    )(slab, t1, t2)
    partner_rows = lax.ppermute(side, "narrow", pair_swap(narrow))
    p2 = pl.pallas_call(
        partner_kernel,
        out_shape=jax.ShapeDtypeStruct(p2.shape, p2.dtype),
        in_specs=[VMEM] * 5,
        out_specs=VMEM,
        compiler_params=params,
        cost_estimate=cost(10**7, 10**5),
    )(partner_rows, p1, p2, t1, t2)
    pooled = pl.pallas_call(
        functools.partial(edge_kernel, narrow),
        out_shape=jax.ShapeDtypeStruct((c2, LANES), jnp.bfloat16),
        in_specs=[VMEM] * 8,
        out_specs=VMEM,
        scratch_shapes=[pltpu.VMEM((rows // 2, width), jnp.float32)],
        compiler_params=params,
        cost_estimate=cost(10**7, 10**5),
    )(crossed_own.reshape(rows // 2, width), crossed_rows, scale, shift, p1, p2, t1, t2)
    pooled_far = lax.ppermute(pooled, BOTH, cross_wide(wide, narrow))
    pooled_pair = lax.ppermute(pooled, "wide", pair_swap(wide))
    mine = jnp.stack([pooled, pooled_pair, pooled_far])[None]
    held, held_places = mine, [0]
    arrivals = [(mine, [0]), (lax.ppermute(mine, "narrow", pair_swap(narrow)), [1])]
    bit = narrow // 2
    while bit > 1:
        other = lax.ppermute(held, "narrow", pair_swap(narrow, bit))
        places = [place ^ bit for place in held_places]
        arrivals.append((other, places))
        arrivals.append(
            (lax.ppermute(other, "narrow", pair_swap(narrow)), [place ^ 1 for place in places])
        )
        if bit > 2:
            held = jnp.concatenate([held, other])
        held_places = held_places + places
        bit //= 2
    total = narrow * LANES
    products = jax.ShapeDtypeStruct((9 * o3, total), jnp.float32)
    z = None
    for group in (arrivals[:2], arrivals[2:-1], arrivals[-1:]):
        if not group:
            continue
        places = [place for _, several in group for place in several]
        operands = [array for array, _ in group] + [t3] + ([] if z is None else [z])
        scratch = [pltpu.VMEM((3 * c2, len(places) * LANES), jnp.bfloat16)]
        common = dict(
            in_specs=[VMEM] * len(operands),
            scratch_shapes=scratch,
            compiler_params=params,
            cost_estimate=cost(10**7, 10**5),
        )
        if group[-1] is not arrivals[-1]:
            z = pl.pallas_call(
                functools.partial(
                    first_products_kernel if z is None else more_products_kernel, places
                ),
                out_shape=products,
                out_specs=VMEM,
                input_output_aliases={} if z is None else {len(operands) - 1: 0},
                **common,
            )(*operands)
        else:
            coarse, _ = pl.pallas_call(
                functools.partial(coarse_kernel, places),
                out_shape=(jax.ShapeDtypeStruct((o3, total), jnp.bfloat16), products),
                out_specs=(VMEM,) * 2,
                input_output_aliases={len(operands) - 1: 1},
                **common,
            )(*operands)
    return coarse[:, None, :]


def solution(mesh):
    in_specs = (P(None, "wide", "narrow", None), P(), P(), P(), P(), P("narrow", None))
    out_specs = P("narrow", "wide", None)
    return jax.shard_map(
        functools.partial(body, mesh.shape["wide"], mesh.shape["narrow"]),
        mesh=mesh,
        in_specs=in_specs,
        out_specs=out_specs,
        check_vma=False,
    )
```

```python
import functools

import jax
import jax.numpy as jnp
from jax import lax
from jax.experimental import pallas as pl
from jax.experimental.pallas import tpu as pltpu
from jax.sharding import PartitionSpec as P

LANES = 128
VMEM = pl.BlockSpec(memory_space=pltpu.VMEM)


def pair_swap(count, bit=1):
    return [(k, k ^ bit) for k in range(count)]


BOTH = ("wide", "narrow")


def crossing(position, count):
    target = position + 1 if position % 2 else position - 1
    return target if 0 <= target < count else None


def cross_wide(wide, narrow):
    bit = 1
    steps = []
    for i in range(wide):
        for j in range(narrow):
            target = crossing(i, wide)
            end = i * narrow + (j ^ bit) if target is None else target * narrow + j
            steps.append((i * narrow + j, end))
    return steps


def cross_narrow(wide, narrow, ends_meet):
    steps = []
    for i in range(wide):
        for j in range(narrow):
            target = crossing(j, narrow)
            if target is None:
                end = i * narrow + narrow - 1 - j if ends_meet else (i ^ 1) * narrow + j
            else:
                end = i * narrow + target
            steps.append((i * narrow + j, end))
    return steps


def weights_kernel(wide, w1_ref, w2_ref, w3_ref, t1_ref, t2_ref, t3_ref):
    i = lax.axis_index("wide")
    keep_low = jnp.where(i == 0, 0.0, 1.0)
    keep_high = jnp.where(i == wide - 1, 0.0, 1.0)

    def kept(value, keep):
        return (value.astype(jnp.float32) * keep).astype(jnp.bfloat16)

    o1 = w1_ref.shape[0]
    c1 = w1_ref.shape[1] // 27
    o2 = w2_ref.shape[0]
    c2 = w2_ref.shape[1] // 27
    o3 = w3_ref.shape[0]
    c3 = w3_ref.shape[1] // 27
    for ref, out, o, c, rows in ((w1_ref, t1_ref, o1, c1, 4), (w2_ref, t2_ref, o2, c2, 2)):
        span = (rows + 2) * c
        for be in range(9):
            taps = [ref[:, (a * 9 + be) * c : (a * 9 + be + 1) * c] for a in range(3)]
            for row in range(rows):
                parts = []
                if row:
                    parts.append(jnp.zeros((o, row * c), jnp.bfloat16))
                parts += taps
                if row < rows - 1:
                    parts.append(jnp.zeros((o, (rows - 1 - row) * c), jnp.bfloat16))
                value = jnp.concatenate(parts, axis=1)
                if rows == 4 and row in (0, 3):
                    value = kept(value, keep_low if row == 0 else keep_high)
                out[row * o : (row + 1) * o, be * span : (be + 1) * span] = value
    for be in range(9):
        for a in range(3):
            value = w3_ref[:, (a * 9 + be) * c3 : (a * 9 + be + 1) * c3]
            if a != 1:
                value = kept(value, keep_low if a == 0 else keep_high)
            t3_ref[be * o3 : (be + 1) * o3, a * c3 : (a + 1) * c3] = value


def shifted(value):
    lane = lax.broadcasted_iota(jnp.int32, value.shape, 1)
    low = jnp.where(lane == 0, 0.0, pltpu.roll(value, 1, 1))
    high = jnp.where(lane == LANES - 1, 0.0, pltpu.roll(value, LANES - 1, 1))
    return low, value, high


def column(row_ref):
    row = row_ref[...]
    square = (row.shape[1], row.shape[1])
    here = lax.broadcasted_iota(jnp.int32, square, 0) == lax.broadcasted_iota(jnp.int32, square, 1)
    return jnp.sum(jnp.where(here, jnp.broadcast_to(row, square), 0.0), axis=1, keepdims=True)


def slab_kernel(
    wide, own_ref, pair_ref, far_ref, scale_ref, shift_ref, out_ref, relay_ref, side_ref, staged
):
    i, j = lax.axis_index("wide"), lax.axis_index("narrow")
    i_odd, j_odd = lax.rem(i, 2), lax.rem(j, 2)
    block, columns = out_ref.shape[0] // 3, out_ref.shape[1]
    c = scale_ref.shape[1]
    depth, height = block // c, columns // LANES
    keep = jnp.where(i == i_odd * (wide - 1), 0.0, 1.0)
    scale, shift = column(scale_ref), column(shift_ref)
    size = own_ref.shape[0]
    for n, ref in enumerate((own_ref, pair_ref, far_ref)):
        staged[n * size : (n + 1) * size, :] = ref[...].astype(jnp.float32)
        slot = (1, 2 - 2 * i_odd, 2 * i_odd)[n]
        gain, offset = (scale * keep, shift * keep) if n == 2 else (scale, shift)
        for d in range(depth):
            for h in range(height):
                start = n * size + d * height + h
                value = staged[pl.ds(start, c, stride=depth * height), :] * gain + offset
                row = slot * block + d * c
                rows = slice(row, row + c) if n == 0 else pl.ds(pl.multiple_of(row, c), c)
                out_ref[rows, h * LANES : (h + 1) * LANES] = value.astype(jnp.bfloat16)

    half = columns // 2
    lane = pl.multiple_of(j_odd * half, half)
    relay_ref[:block, :] = out_ref[:block, pl.ds(lane, half)]
    relay_ref[block:, :] = out_ref[2 * block :, pl.ds(lane, half)]
    side_ref[...] = out_ref[:, pl.ds(pl.multiple_of((1 - j_odd) * half, half), half)]


def dot(a, b):
    return jnp.dot(a, b, preferred_element_type=jnp.float32)


def tile(ref, *picks):
    return jnp.concatenate([ref[:, k * LANES : (k + 1) * LANES] for k in picks], axis=1)


def spread(value, ref, at):
    rows, columns = value.shape
    for k in range(columns // LANES):
        parts = shifted(value[:, k * LANES : (k + 1) * LANES].astype(jnp.float32))
        for e, part in enumerate(parts):
            ref[e * rows : (e + 1) * rows, pl.ds(at + k * LANES, LANES)] = part.astype(jnp.bfloat16)


def thirds(ref):
    span = ref.shape[1] // 3
    return [ref[:, b * span : (b + 1) * span] for b in range(3)]


def beside(*parts):
    return jnp.concatenate(parts, axis=1)


def part(ref, k):
    return ref[:, k * LANES : (k + 1) * LANES]


def centre_kernel(x_ref, w1_ref, w2_ref, p1_ref, p2_ref):
    taps = [stacked(part(x_ref, k).astype(jnp.float32)) for k in range(4)]
    first = thirds(w1_ref)
    pairs = jnp.concatenate([beside(taps[b], taps[b + 1]) for b in range(3)], axis=0)
    inner = jnp.maximum(dot(w1_ref[...], pairs), 0.0)
    both = beside(stacked(inner[:, :LANES]), stacked(inner[:, LANES:]))
    r0 = dot(first[0], beside(taps[2], taps[3]))
    r1 = dot(first[1], beside(taps[0], taps[3]))
    r2 = dot(first[2], beside(taps[0], taps[1]))
    p1_ref[:, 0:LANES] = r2[:, :LANES]
    p1_ref[:, LANES : 2 * LANES] = r2[:, LANES:] + r1[:, :LANES]
    p1_ref[:, 2 * LANES : 3 * LANES] = r0[:, LANES:]
    p1_ref[:, 3 * LANES :] = r1[:, LANES:] + r0[:, :LANES]
    q0, q1, q2 = (dot(w, both) for w in thirds(w2_ref))
    p2_ref[:, 0:LANES] = q2[:, :LANES]
    p2_ref[:, LANES : 2 * LANES] = q2[:, LANES:] + q1[:, :LANES]
    p2_ref[:, 2 * LANES : 3 * LANES] = q0[:, LANES:]
    p2_ref[:, 3 * LANES :] = q1[:, LANES:] + q0[:, :LANES]


def stacked(value):
    return jnp.concatenate([part.astype(jnp.bfloat16) for part in shifted(value)], axis=0)


def side_terms(high, keep, feature, p1_ref, w1_ref, w2_ref):
    span1, span2 = w1_ref.shape[1] // 3, w2_ref.shape[1] // 3
    outer1, outer2 = pl.multiple_of(2 * high * span1, LANES), pl.multiple_of(2 * high * span2, LANES)
    taps = jnp.concatenate([stacked(feature(k)) for k in range(2)], axis=1)
    r = dot(w1_ref[:, pl.ds(outer1, span1)], taps)
    r1 = dot(w1_ref[:, span1 : 2 * span1], taps)
    up = high == 1
    before = p1_ref[:, pl.ds(pl.multiple_of(high * 2 * LANES, LANES), 2 * LANES)]
    end = jnp.where(up, r[:, LANES:] + r1[:, :LANES], r[:, :LANES] + r1[:, LANES:])
    end = jnp.maximum(end + before[:, :LANES], 0.0)
    end = stacked(end if keep is None else end * keep)
    near = jnp.where(up, r[:, :LANES], r[:, LANES:])
    near = stacked(jnp.maximum(near + before[:, LANES:], 0.0))
    q = dot(w2_ref[:, pl.ds(outer2, span2)], jnp.concatenate([end, near], axis=1))
    q1 = dot(w2_ref[:, span2 : 2 * span2], near)
    return q[:, :LANES] + q1, q[:, LANES:]


def partner_kernel(rows_ref, p1_ref, p2_ref, w1_ref, w2_ref, out_ref):
    high = 1 - lax.rem(lax.axis_index("narrow"), 2)

    def feature(k):
        return rows_ref[:, k * LANES : (k + 1) * LANES].astype(jnp.float32)

    end, near = side_terms(high, None, feature, p1_ref, w1_ref, w2_ref)
    at = pl.multiple_of(high * 2 * LANES, LANES)
    out_ref[...] = p2_ref[...]
    out_ref[:, pl.ds(at, LANES)] += end
    out_ref[:, pl.ds(at + LANES, LANES)] += near


def edge_kernel(
    narrow, own_ref, rows_ref, scale_ref, shift_ref, p1_ref, p2_ref, w1_ref, w2_ref, out_ref, staged
):
    j = lax.axis_index("narrow")
    high = lax.rem(j, 2)
    keep = jnp.where(j == high * (narrow - 1), 0.0, 1.0)
    staged[...] = own_ref[...].astype(jnp.float32)
    scale, shift = column(scale_ref) * keep, column(shift_ref) * keep
    c = scale.shape[0]

    def feature(k):
        rows = rows_ref[:, k * LANES : (k + 1) * LANES].astype(jnp.float32) * keep
        own = [staged[pl.ds(2 * d + k, c, stride=4), :] * scale + shift for d in range(2)]
        return jnp.concatenate([rows[: 2 * c]] + own + [rows[2 * c :]], axis=0)

    end, near = side_terms(high, keep, feature, p1_ref, w1_ref, w2_ref)
    c2 = out_ref.shape[0]
    at = pl.multiple_of(high * 2 * LANES, LANES)
    other = pl.multiple_of((1 - high) * 2 * LANES, LANES)

    def best(one, two):
        value = jnp.maximum(one, two)
        value = jnp.maximum(jnp.maximum(value[:c2], value[c2:]), 0.0)
        return jnp.maximum(value, pltpu.roll(value, LANES - 1, 1)).astype(jnp.bfloat16)

    mine = best(end + p2_ref[:, pl.ds(at, LANES)], near + p2_ref[:, pl.ds(at + LANES, LANES)])
    rest = best(p2_ref[:, pl.ds(other, LANES)], p2_ref[:, pl.ds(other + LANES, LANES)])
    cell = lax.broadcasted_iota(jnp.int32, (2 * LANES, LANES), 0)
    target = lax.broadcasted_iota(jnp.int32, (2 * LANES, LANES), 1)
    wanted = jnp.bitwise_xor(2 * target, high * LANES)
    pick = (cell == wanted).astype(jnp.bfloat16)
    out_ref[...] = dot(jnp.concatenate([mine, rest], axis=1), pick).astype(jnp.bfloat16)


def coarse_products(places, blocks, w3_ref, z_ref, slab):
    i, j = lax.axis_index("wide"), lax.axis_index("narrow")
    i_odd = lax.rem(i, 2)
    slots = (1, 2 - 2 * i_odd, 2 * i_odd)
    at = 0
    for ref in blocks:
        for r in range(ref.shape[0]):
            for k in range(3):
                row = pl.multiple_of(slots[k] * ref.shape[2], ref.shape[2])
                slab[pl.ds(row, ref.shape[2]), at : at + LANES] = ref[r, k]
            at += LANES
    z = dot(w3_ref[...], slab[...])
    for k, place in enumerate(places):
        lane = pl.multiple_of(jnp.bitwise_xor(j, place) * LANES, LANES)
        z_ref[:, pl.ds(lane, LANES)] = z[:, k * LANES : (k + 1) * LANES]


def first_products_kernel(places, *refs):
    *blocks, w3_ref, z_ref, slab = refs
    coarse_products(places, blocks, w3_ref, z_ref, slab)


def more_products_kernel(places, *refs):
    *blocks, w3_ref, _, z_ref, slab = refs
    coarse_products(places, blocks, w3_ref, z_ref, slab)


def coarse_kernel(places, blocks_ref, w3_ref, before_ref, out_ref, z_ref, slab):
    del before_ref
    coarse_products(places, [blocks_ref], w3_ref, z_ref, slab)
    o, total = out_ref.shape
    width = LANES // 2
    count = total // LANES
    lane = lax.broadcasted_iota(jnp.int32, (o, LANES), 1)
    column_of = lax.rem(lane, width)

    def z(b, e, q):
        if q < 0 or q >= count:
            return jnp.zeros((o, LANES), jnp.float32)
        at = (b * 3 + e) * o
        return z_ref[at : at + o, q * LANES : (q + 1) * LANES]

    for q in range(count):
        terms = []
        for e in range(3):
            crossed = jnp.where(
                lane < width, z(0, e, q) + z(2, e, q + 1), z(0, e, q - 1) + z(2, e, q)
            )
            terms.append(z(1, e, q) + pltpu.roll(crossed, width, 1))
        low = jnp.where(column_of == 0, 0.0, pltpu.roll(terms[0], 1, 1))
        high = jnp.where(column_of == width - 1, 0.0, pltpu.roll(terms[2], LANES - 1, 1))
        out_ref[:, q * LANES : (q + 1) * LANES] = jnp.maximum(low + terms[1] + high, 0.0).astype(
            jnp.bfloat16
        )


def body(
    wide, narrow, stored_features, channel_scale, channel_shift, first_weight, second_weight,
    third_weight,
):
    c1, depth, height, width = stored_features.shape
    c2 = second_weight.shape[0]
    o3 = third_weight.shape[0]
    params = pltpu.CompilerParams(vmem_limit_bytes=24 * 1024 * 1024)
    rows = c1 * depth * height
    columns = height * width
    scale, shift = channel_scale.reshape(1, c1), channel_shift.reshape(1, c1)

    def cost(flops, size):
        return pl.CostEstimate(flops=flops, bytes_accessed=size, transcendentals=0)

    far = lax.ppermute(stored_features, BOTH, cross_wide(wide, narrow))
    pair = lax.ppermute(stored_features, "wide", pair_swap(wide))
    t1, t2, t3 = pl.pallas_call(
        functools.partial(weights_kernel, wide),
        out_shape=(
            jax.ShapeDtypeStruct((4 * c1, 9 * 6 * c1), jnp.bfloat16),
            jax.ShapeDtypeStruct((2 * c2, 9 * 4 * c1), jnp.bfloat16),
            jax.ShapeDtypeStruct((9 * o3, 3 * c2), jnp.bfloat16),
        ),
        in_specs=[VMEM] * 3,
        out_specs=(VMEM,) * 3,
        compiler_params=params,
        cost_estimate=cost(10**6, 4 * 10**6),
    )(first_weight, second_weight, third_weight)
    half = height // 2
    edges = lax.dynamic_slice_in_dim(
        stored_features, lax.axis_index("narrow") % 2 * half, half, axis=2
    )
    crossed_own = lax.ppermute(edges, BOTH, cross_narrow(wide, narrow, True))
    pair, raw, scale, shift = lax.optimization_barrier((pair, stored_features, scale, shift))
    pair_rows = pair.reshape(rows, width)
    far, pair_rows, t1, t2, t3 = lax.optimization_barrier((far, pair_rows, t1, t2, t3))
    slab, relay, side = pl.pallas_call(
        functools.partial(slab_kernel, wide),
        out_shape=(
            jax.ShapeDtypeStruct((6 * c1, columns), jnp.bfloat16),
            jax.ShapeDtypeStruct((4 * c1, columns // 2), jnp.bfloat16),
            jax.ShapeDtypeStruct((6 * c1, columns // 2), jnp.bfloat16),
        ),
        in_specs=[VMEM] * 5,
        out_specs=(VMEM,) * 3,
        scratch_shapes=[pltpu.VMEM((3 * rows, width), jnp.float32)],
        compiler_params=params,
        cost_estimate=cost(10**6, 2 * 10**6),
    )(raw.reshape(rows, width), pair_rows, far.reshape(rows, width), scale, shift)
    relay, side, crossed_own = lax.optimization_barrier((relay, side, crossed_own))
    crossed_rows = lax.ppermute(relay, BOTH, cross_narrow(wide, narrow, False))
    p1, p2 = pl.pallas_call(
        centre_kernel,
        out_shape=(
            jax.ShapeDtypeStruct((4 * c1, 4 * width), jnp.float32),
            jax.ShapeDtypeStruct((2 * c2, 4 * width), jnp.float32),
        ),
        in_specs=[VMEM] * 3,
        out_specs=(VMEM,) * 2,
        compiler_params=params,
        cost_estimate=cost(10**7, 10**5),
    )(slab, t1, t2)
    partner_rows = lax.ppermute(side, "narrow", pair_swap(narrow))
    p2 = pl.pallas_call(
        partner_kernel,
        out_shape=jax.ShapeDtypeStruct(p2.shape, p2.dtype),
        in_specs=[VMEM] * 5,
        out_specs=VMEM,
        compiler_params=params,
        cost_estimate=cost(10**7, 10**5),
    )(partner_rows, p1, p2, t1, t2)
    pooled = pl.pallas_call(
        functools.partial(edge_kernel, narrow),
        out_shape=jax.ShapeDtypeStruct((c2, LANES), jnp.bfloat16),
        in_specs=[VMEM] * 8,
        out_specs=VMEM,
        scratch_shapes=[pltpu.VMEM((rows // 2, width), jnp.float32)],
        compiler_params=params,
        cost_estimate=cost(10**7, 10**5),
    )(crossed_own.reshape(rows // 2, width), crossed_rows, scale, shift, p1, p2, t1, t2)
    pooled_far = lax.ppermute(pooled, BOTH, cross_wide(wide, narrow))
    pooled_pair = lax.ppermute(pooled, "wide", pair_swap(wide))
    mine = jnp.stack([pooled, pooled_pair, pooled_far])[None]
    held, held_places = mine, [0]
    arrivals = [(mine, [0]), (lax.ppermute(mine, "narrow", pair_swap(narrow)), [1])]
    bit = narrow // 2
    while bit > 1:
        other = lax.ppermute(held, "narrow", pair_swap(narrow, bit))
        places = [place ^ bit for place in held_places]
        arrivals.append((other, places))
        arrivals.append(
            (lax.ppermute(other, "narrow", pair_swap(narrow)), [place ^ 1 for place in places])
        )
        if bit > 2:
            held = jnp.concatenate([held, other])
        held_places = held_places + places
        bit //= 2
    total = narrow * LANES
    products = jax.ShapeDtypeStruct((9 * o3, total), jnp.float32)
    z = None
    for group in (arrivals[:2], arrivals[2:-1], arrivals[-1:]):
        if not group:
            continue
        places = [place for _, several in group for place in several]
        operands = [array for array, _ in group] + [t3] + ([] if z is None else [z])
        scratch = [pltpu.VMEM((3 * c2, len(places) * LANES), jnp.bfloat16)]
        common = dict(
            in_specs=[VMEM] * len(operands),
            scratch_shapes=scratch,
            compiler_params=params,
            cost_estimate=cost(10**7, 10**5),
        )
        if group[-1] is not arrivals[-1]:
            z = pl.pallas_call(
                functools.partial(
                    first_products_kernel if z is None else more_products_kernel, places
                ),
                out_shape=products,
                out_specs=VMEM,
                input_output_aliases={} if z is None else {len(operands) - 1: 0},
                **common,
            )(*operands)
        else:
            coarse, _ = pl.pallas_call(
                functools.partial(coarse_kernel, places),
                out_shape=(jax.ShapeDtypeStruct((o3, total), jnp.bfloat16), products),
                out_specs=(VMEM,) * 2,
                input_output_aliases={len(operands) - 1: 1},
                **common,
            )(*operands)
    return coarse[:, None, :]


def solution(mesh):
    in_specs = (P(None, "wide", "narrow", None), P(), P(), P(), P(), P("narrow", None))
    out_specs = P("narrow", "wide", None)
    return jax.shard_map(
        functools.partial(body, mesh.shape["wide"], mesh.shape["narrow"]),
        mesh=mesh,
        in_specs=in_specs,
        out_specs=out_specs,
        check_vma=False,
    )
```
